32 devices in a mesh: groups: 2 (over y), space: 4 (over z), test: 4 (over x, core).
Axes of the slice: x: 2, y: 2, z: 4, core: 2. Of those that a mesh axis runs over, the one named last changes fastest.
Arguments:
- log_k: bfloat16 [384, 288, 128], P(('groups', 'space')), parts along dimension 0, may hold values from -1.5 to 1.5
- heads: bfloat16 [4, 384, 288, 128], P('test', ('groups', 'space')), parts along dimension 1, may hold values from -6 to 6
- warm_adjoint: bfloat16 [4, 384, 288, 128], P('test', ('groups', 'space')), parts along dimension 1, may hold values from -6 to 6
- obs_columns: int32 [4, 128], P('test', 'groups'), parts along dimension 1, may hold values from 0 to 55295
- obs_residuals: float32 [4, 128, 128], P('test', 'groups'), parts along dimension 1, may hold values from -18 to 18
- well_columns: int32 [8], P(('groups', 'test')), parts along dimension 0, may hold values from 0 to 55295
Outputs:
- prior_gradient: float32 [384, 288, 128], P(('groups', 'space'), 'test'), parts along dimension 0
The draws below stay inside these ranges and needn't reach their ends.
There are 2 independent parts, one for each index of `groups`. The reference program is written for one: setup_inputs(seed, part) draws one part's arguments, and reference() takes and returns one part's arrays. A program takes and returns all parts, laid end to end along the dimension named above; each array names one. Nothing has to cross between parts.
Inputs may be any that keep to these rules, and one draw needn't show every extreme that they name: `obs_columns`: x * 288 + y of the borehole's cell column. `well_columns`: x * 288 + y of the well's cell column.
All inputs are finite; a program needn't handle non-finite values.
Results may differ from the reference program's by a relative error of at most 0.0003.
Values may be sent and summed in bfloat16 or wider, within the bound.
A program may use at most 128 MiB of HBM per device.

```python
import jax
import jax.numpy as jnp

NX = 192
NY = 288
NZ = 128
OBS = 64
ITERS = 2
TESTS = 4


def plant(array, key, least, largest):
    index_at = [jax.random.randint(jax.random.fold_in(key, axis), (), 0, length) for axis, length in enumerate(array.shape)]
    widest = array.shape.index(max(array.shape))
    neighbour = index_at[:widest] + [(index_at[widest] + 1) % array.shape[widest]] + index_at[widest + 1:]
    return array.at[tuple(index_at)].set(least).at[tuple(neighbour)].set(largest)


def block_scale(key, shape, pieces, least, top_value):
    def one(position, shards_of):
        steps = jax.random.uniform(jax.random.fold_in(jax.random.fold_in(key, 6), position), (shards_of,), jnp.float32, least / len(pieces), top_value / len(pieces))
        return jnp.repeat(jnp.exp(steps), shape[position] // shards_of).reshape((-1,) + (1,) * (len(shape) - position - 1))

    level = one(*pieces[0])
    for cut in pieces[1:]:
        level = level * one(*cut)
    return level


def bell_draw(rng, shape, scale, bound, shards=(), held_as=jnp.bfloat16):
    entries = jax.random.normal(rng, shape, jnp.float32) * scale
    if len(shards) > 0:
        entries = block_scale(rng, shape, shards, -0.22, 0.18) * entries
    return jnp.clip(entries, min=-bound, max=bound).astype(held_as)


def setup_inputs(seed: int = 0, part: int = 0) -> dict:
    key_of = jax.random.split(jax.random.key(seed), 7)
    part_keys = jax.random.split(jax.random.fold_in(key_of[6], part), 7)
    return {
        "log_k": jnp.clip(jax.random.uniform(part_keys[0], (NX, NY, NZ), jnp.float32, -1.5, 1.5) * block_scale(part_keys[0], (NX, NY, NZ), ((0, 4),), -0.4, 0.0), -1.5, 1.5).astype(jnp.bfloat16),
        "heads": bell_draw(part_keys[1], (TESTS, NX, NY, NZ), 1.0, 6.0, ((0, 4), (1, 4))),
        "warm_adjoint": bell_draw(part_keys[2], (TESTS, NX, NY, NZ), 1.0, 6.0, ((0, 4), (1, 4))),
        "obs_columns": plant(jax.random.randint(part_keys[3], (TESTS, OBS), 0, NX * NY), jax.random.fold_in(part_keys[3], 1), 0, (NX * NY) - 1).astype(jnp.int32),
        "obs_residuals": bell_draw(part_keys[4], (TESTS, OBS, NZ), 3.0, 18.0, ((0, 4),), jnp.float32),
        "well_columns": plant(jax.random.randint(part_keys[5], (TESTS,), 0, NX * NY), jax.random.fold_in(part_keys[5], 1), 0, (NX * NY) - 1).astype(jnp.int32),
    }


prior_gain = 5.0
range_squared = 4.0


def neighbours(padded):
    return [padded[2:, 1:-1, 1:-1], padded[:-2, 1:-1, 1:-1], padded[1:-1, 2:, 1:-1],
            padded[1:-1, :-2, 1:-1], padded[1:-1, 1:-1, 2:], padded[1:-1, 1:-1, :-2]]


def operate(values, padded, conduct):
    summed = jnp.zeros_like(values)
    for face_k, beside in zip(conduct, neighbours(padded)):
        summed = summed + face_k * (values - beside)
    return summed


def kappa_of(indices, length):
    return 4.0 * jnp.sin(jnp.pi * indices / length) ** 2


def reference(log_k, heads, warm_adjoint, obs_columns, obs_residuals, well_columns):
    logk_val = log_k.astype(jnp.float32)
    conduct = [jnp.exp(0.5 * (logk_val + beside)) for beside in neighbours(jnp.pad(logk_val, 1))]
    summed = jnp.zeros((NX, NY, NZ), jnp.float32)
    column_ids = jnp.arange(NX * NY, dtype=jnp.int32).reshape(NX, NY)
    for test_id in range(TESTS):
        source = jnp.zeros((NX * NY, NZ), jnp.float32).at[obs_columns[test_id]].add(obs_residuals[test_id])
        source = source.reshape(NX, NY, NZ)
        adjoint = warm_adjoint[test_id].astype(jnp.float32)
        residual = source - operate(adjoint, jnp.pad(adjoint, 1), conduct)
        direction = residual
        norm_now = jnp.sum(residual * residual)
        for iteration in range(ITERS):
            applied = operate(direction, jnp.pad(direction, 1), conduct)
            step_length = norm_now / jnp.sum(direction * applied)
            adjoint = adjoint + step_length * direction
            if iteration + 1 < ITERS:
                residual = residual - step_length * applied
                norm_next = jnp.sum(residual * residual)
                direction = residual + (norm_next / norm_now) * direction
                norm_now = norm_next
        head_val = heads[test_id].astype(jnp.float32)
        misfit_term = jnp.zeros_like(adjoint)
        for face_k, lam_side, head_side in zip(conduct, neighbours(jnp.pad(adjoint, 1)), neighbours(jnp.pad(head_val, 1))):
            misfit_term = misfit_term + face_k * (adjoint - lam_side) * (head_val - head_side)
        keep_mask = (column_ids != well_columns[test_id]).astype(jnp.float32)
        summed = summed + (-0.5 * misfit_term * keep_mask[:, :, None])
    kappa_x = kappa_of(jnp.arange(NX).astype(jnp.float32), NX)
    kappa_y = kappa_of(jnp.arange(NY).astype(jnp.float32), NY)
    kappa_z = kappa_of(jnp.arange(NZ).astype(jnp.float32), NZ)
    spectrum = prior_gain / (1.0 + range_squared * (kappa_x[:, None, None] + kappa_y[None, :, None] + kappa_z[None, None, :])) ** 2
    result = jnp.real(jnp.fft.ifftn(jnp.fft.fftn(summed) * spectrum))
    return result.astype(jnp.float32)
```

```python
import functools

import jax
import jax.numpy as jnp
from jax import lax
from jax.experimental import pallas as pl
from jax.experimental.pallas import tpu as pltpu
from jax.sharding import PartitionSpec as P

ITERS = 2


prior_gain = 5.0
range_squared = 4.0


def with_halo(cells, sides, width):
    for axis, dim in sides:
        count = lax.axis_size(axis)
        ends = count - 1
        head = lax.slice_in_dim(cells, 0, width, axis=dim)
        tail = lax.slice_in_dim(cells, cells.shape[dim] - width, cells.shape[dim], axis=dim)
        cells = jnp.concatenate(
            [
                lax.ppermute(tail, axis, [(i, (i + 1) % count) for i in range(ends)]),
                cells,
                lax.ppermute(head, axis, [((i + 1) % count, i) for i in range(ends)]),
            ],
            axis=dim,
        )
    return cells


def neighbours(padded):
    return [
        padded[2:, 1:-1, 1:-1],
        padded[:-2, 1:-1, 1:-1],
        padded[1:-1, 2:, 1:-1],
        padded[1:-1, :-2, 1:-1],
        padded[1:-1, 1:-1, 2:],
        padded[1:-1, 1:-1, :-2],
    ]


def operate(values, padded, conduct):
    summed = jnp.zeros_like(values)
    for face_k, beside in zip(conduct, neighbours(padded)):
        summed = summed + face_k * (values - beside)
    return summed


def kappa_of(indices, length):
    return 4.0 * jnp.sin(jnp.pi * indices / length) ** 2


def pad_sides(padded):
    return jnp.pad(padded, ((0, 0), (1, 1), (1, 1)))


def with_faces(values):
    return pad_sides(with_halo(values, (("space", 0),), 1))


def squares(residual):
    return lax.psum(jnp.sum(residual * residual), "space")


def hartley(length):
    indices = jnp.arange(length, dtype=jnp.int32)
    products = indices[:, None] * indices[None, :] % length
    angles = products.astype(jnp.float32) * (2.0 * jnp.pi / length)
    return jnp.cos(angles) + jnp.sin(angles)


def on_device(log_k, heads, warm_adjoint, obs_columns, obs_residuals, well_columns):
    slab_rows, width_cells, depth_cells = log_k.shape
    space_count = lax.axis_size("space")
    first_row = lax.axis_index("space") * slab_rows
    logk_pad, head_pad = (
        with_halo(log_k, (("space", 0),), 1),
        with_halo(heads[0], (("space", 0),), 1),
    )
    logk_val = log_k.astype(jnp.float32)
    conduct = [
        jnp.exp(0.5 * (logk_val + beside))
        for beside in neighbours(pad_sides(logk_pad.astype(jnp.float32)))
    ]
    columns = obs_columns[0]
    row_local = columns // width_cells - first_row
    inside = (row_local >= 0) & (row_local < slab_rows)
    row_local = jnp.where(inside, row_local, slab_rows)
    source = jnp.zeros((slab_rows, width_cells, depth_cells), jnp.float32)
    source = source.at[row_local, columns % width_cells].add(obs_residuals[0], mode="drop")
    adjoint = warm_adjoint[0].astype(jnp.float32)
    lam_padded = with_faces(adjoint)
    residual = source - operate(adjoint, lam_padded, conduct)
    direction = residual
    norm_now = squares(residual)
    for iteration in range(ITERS):
        dir_padded = with_faces(direction)
        applied = operate(direction, dir_padded, conduct)
        step_length = norm_now / lax.psum(jnp.sum(direction * applied), "space")
        adjoint = adjoint + step_length * direction
        lam_padded = lam_padded + step_length * dir_padded
        if iteration + 1 < ITERS:
            residual = residual - step_length * applied
            norm_next = squares(residual)
            direction = residual + norm_next / norm_now * direction
            norm_now = norm_next
    lam_full = pad_sides(with_halo(adjoint, (("space", 0),), 1))
    head_val = heads[0].astype(jnp.float32)
    misfit_term = jnp.zeros_like(adjoint)
    for face_k, lam_side, head_side in zip(
        conduct, neighbours(lam_full), neighbours(pad_sides(head_pad.astype(jnp.float32)))
    ):
        misfit_term = misfit_term + face_k * (adjoint - lam_side) * (head_val - head_side)
    column_ids = (first_row + jnp.arange(slab_rows, dtype=jnp.int32))[
        :, None
    ] * width_cells + jnp.arange(width_cells, dtype=jnp.int32)[None, :]
    keep_mask = (column_ids != well_columns[0]).astype(jnp.float32)
    partial_value = -0.5 * misfit_term * keep_mask[:, :, None]
    highest = lax.Precision.HIGHEST
    cas_depth = hartley(depth_cells)
    cas_across = hartley(width_cells)
    along_cells = slab_rows * space_count
    cas_along = hartley(along_cells)
    summed = lax.psum_scatter(partial_value, "test", scatter_dimension=1, tiled=True)
    depth_freq = jnp.einsum("xyz,zk->xky", summed, cas_depth, precision=highest)
    pencil = lax.all_to_all(depth_freq, "test", split_axis=1, concat_axis=2, tiled=True)
    across_freq = jnp.einsum("xzy,yk->kzx", pencil, cas_across, precision=highest)
    column_block = lax.all_to_all(across_freq, "space", split_axis=0, concat_axis=2, tiled=True)
    along_freq = jnp.einsum("yzx,xk->yzk", column_block, cas_along, precision=highest)
    across_rows = column_block.shape[0]
    depth_rows = column_block.shape[1]
    kappa_x = kappa_of(jnp.arange(along_cells).astype(jnp.float32), along_cells)
    kappa_y = kappa_of(
        (lax.axis_index("space") * across_rows + jnp.arange(across_rows)).astype(jnp.float32),
        width_cells,
    )
    kappa_z = kappa_of(
        (lax.axis_index("test") * depth_rows + jnp.arange(depth_rows)).astype(jnp.float32),
        depth_cells,
    )
    spectrum = (
        prior_gain
        / (
            1.0
            + range_squared
            * (kappa_y[:, None, None] + kappa_z[None, :, None] + kappa_x[None, None, :])
        )
        ** 2
    )
    along_back = jnp.einsum("yzk,kx->yzx", along_freq * spectrum, cas_along, precision=highest)
    slab_block = lax.all_to_all(along_back, "space", split_axis=2, concat_axis=0, tiled=True)
    across_back = jnp.einsum("yzx,yk->xzk", slab_block, cas_across, precision=highest)
    depth_block = lax.all_to_all(across_back, "test", split_axis=2, concat_axis=1, tiled=True)
    result = jnp.einsum("xky,kz->xyz", depth_block, cas_depth, precision=highest)
    scale_back = 1.0 / (along_cells * width_cells * depth_cells)
    return result * scale_back


HIGHEST = lax.Precision.HIGHEST
VM = pl.BlockSpec(memory_space=pltpu.VMEM)
SM = pl.BlockSpec(memory_space=pltpu.SMEM)
BIG = pltpu.CompilerParams(vmem_limit_bytes=60 * 1024 * 1024)


def shape(*dims, dtype=jnp.float32):
    return jax.ShapeDtypeStruct(dims, dtype)


def iotas(plane):
    return (
        lax.broadcasted_iota(jnp.int32, plane, 0),
        lax.broadcasted_iota(jnp.int32, plane, 1),
    )


def ring_sum(plane, edge):
    rows, lanes = plane.shape
    at_row, at_lane = iotas(plane.shape)
    up = jnp.where(at_row == rows - 1, edge, pltpu.roll(plane, rows - 1, 0))
    down = jnp.where(at_row == 0, edge, pltpu.roll(plane, 1, 0))
    right = jnp.where(at_lane == lanes - 1, edge, pltpu.roll(plane, lanes - 1, 1))
    left = jnp.where(at_lane == 0, edge, pltpu.roll(plane, 1, 1))
    return (up + down) + (right + left)


def plane_total(plane):
    rows, lanes = plane.shape
    return jnp.sum(plane.reshape(rows // 8, 8, lanes), axis=0)


def swap_blocks(planes):
    count = len(planes)
    lanes = planes[0].shape[1]
    block = lanes // count
    at_lane = iotas(planes[0].shape)[1] // block
    swapped = []
    for to in range(count):
        joined = planes[to]
        for frm in range(count):
            if frm != to:
                shift = (block * (frm - to)) % lanes
                joined = jnp.where(at_lane == frm, pltpu.roll(planes[frm], shift, 1), joined)
        swapped.append(joined)
    return swapped


def residual_kernel(
    spot, columns, logk, warm, before, after, observed, start, image, soft, around, sums, weighted
):
    rows, width, depth = logk.shape
    first_row, last_row = spot[0], spot[1]

    def prepare(to, logk_row, warm_row):
        soft_row = jnp.exp(0.5 * logk_row.astype(jnp.float32))
        soft[to] = soft_row
        weighted[to] = soft_row * warm_row.astype(jnp.float32)

    for i in range(3):
        prepare(i, before[i], before[3 + i])
        prepare(rows + 3 + i, after[i], after[3 + i])

    def fill(i, _):
        prepare(i + 3, logk[i], warm[i])
        return 0

    lax.fori_loop(0, rows, fill, 0)

    def first(i, _):
        row = first_row + i - 2
        inside = ((row >= 0) & (row < last_row)).astype(jnp.float32)
        soft_row = soft[i + 1]
        near = ring_sum(soft_row, 1.0) + (soft[i] + soft[i + 2])
        around[i] = near
        held = weighted[i + 1]
        beside = ring_sum(held, 0.0) + (weighted[i] + weighted[i + 2])
        start[i] = (soft_row * beside - held * near) * inside
        return 0

    lax.fori_loop(0, rows + 4, first, 0)

    def add(o, _):
        column = columns[0, o]
        row = column // width
        place = column - row * width
        local = row - first_row + 2

        @pl.when((local >= 0) & (local < rows + 4))
        def _():
            start[local, pl.ds(place, 1), :] += observed[pl.ds(o, 1), :]

        return 0

    lax.fori_loop(0, columns.shape[1], add, 0)

    def scale(i, _):
        weighted[i] = soft[i + 1] * start[i]
        return 0

    lax.fori_loop(0, rows + 4, scale, 0)

    def second(i, carry):
        total_rr, total_rq = carry
        row = first_row + i - 1
        inside = ((row >= 0) & (row < last_row)).astype(jnp.float32)
        held = weighted[i + 1]
        beside = ring_sum(held, 0.0) + (weighted[i] + weighted[i + 2])
        applied = (held * around[i + 1] - soft[i + 2] * beside) * inside
        image[i] = applied
        value = start[i + 1]
        own = ((i >= 1) & (i <= rows)).astype(jnp.float32)
        return (
            total_rr + own * plane_total(value * value),
            total_rq + own * plane_total(value * applied),
        )

    zero = jnp.zeros((8, depth), jnp.float32)
    total_rr, total_rq = lax.fori_loop(0, rows + 2, second, (zero, zero))
    sums[0] = total_rr
    sums[1] = total_rq


def second_kernel(scalars, start, image, soft, around, sums, weighted):
    rows = start.shape[0] - 4
    step = scalars[0]

    def scale(i, _):
        weighted[i] = soft[i + 2] * (start[i + 1] - step * image[i])
        return 0

    lax.fori_loop(0, rows + 2, scale, 0)

    def apply(i, carry):
        total_rr, total_rq = carry
        held = weighted[i + 1]
        beside = ring_sum(held, 0.0) + (weighted[i] + weighted[i + 2])
        value = start[i + 2] - step * image[i + 1]
        applied = held * around[i + 2] - soft[i + 3] * beside
        return total_rr + plane_total(value * value), total_rq + plane_total(value * applied)

    zero = jnp.zeros((8, start.shape[2]), jnp.float32)
    total_rr, total_rq = lax.fori_loop(0, rows, apply, (zero, zero))
    sums[0] = total_rr
    sums[1] = total_rq


def face_terms(soft, field, head, axis):
    size = soft.shape[axis]
    at = iotas(soft.shape)[axis]
    both = field * head
    ahead = size - 1
    product = (field - pltpu.roll(field, ahead, axis)) * (head - pltpu.roll(head, ahead, axis))
    upper = jnp.where(at == size - 1, both, pltpu.roll(soft, ahead, axis) * product)
    lower = jnp.where(at == 0, both, pltpu.roll(soft * product, 1, axis))
    return upper + lower


def gradient_kernel(
    spot, scalars, warm, heads, before, after, start, image, soft, cas, out, field, head
):
    rows, width, depth = warm.shape
    first_row = spot[0]
    well = spot[2]
    with_start, with_image = scalars[0], scalars[1]

    def fill(to, warm_row, head_row):
        field[to] = (
            warm_row.astype(jnp.float32) + with_start * start[to + 1] - with_image * image[to]
        )
        head[to] = head_row.astype(jnp.float32)

    fill(0, before[5], before[6])
    fill(rows + 1, after[3], after[6])

    def middle(i, _):
        fill(i + 1, warm[i], heads[i])
        return 0

    lax.fori_loop(0, rows, middle, 0)
    at_row = iotas((width, depth))[0]
    count = out.shape[0]

    def term(i):
        s, f, h = soft[i + 3], field[i + 1], head[i + 1]
        gathered = face_terms(s, f, h, 0) + face_terms(s, f, h, 1)
        gathered += soft[i + 2] * ((f - field[i]) * (h - head[i]))
        gathered += soft[i + 4] * ((f - field[i + 2]) * (h - head[i + 2]))
        keep = at_row != well - (first_row + i) * width
        value = jnp.where(keep, -0.5 * s * gathered, 0.0)
        return jnp.dot(value, cas[...], precision=HIGHEST, preferred_element_type=jnp.float32)

    def group(g, _):
        for t, plane in enumerate(swap_blocks([term(g * count + p) for p in range(count)])):
            out[t, g] = plane
        return 0

    lax.fori_loop(0, rows // count, group, 0)


def moment_kernel(count, summed, cas, rho, freq, moments):
    groups, width, lanes = summed.shape
    part = width // count

    def across(g, _):
        mixed = jnp.dot(cas[...], summed[g], precision=HIGHEST, preferred_element_type=jnp.float32)
        blocks = [mixed[j * part : (j + 1) * part] for j in range(count)]
        for p, plane in enumerate(swap_blocks(blocks)):
            freq[g * count + p] = plane
        return 0

    lax.fori_loop(0, groups, across, 0)
    pole = rho[...]
    rows = groups * count

    def walk(i, carry):
        one, two, back_one, back_two = carry
        value, back = freq[i], freq[rows - 1 - i]
        return (
            value + pole * one,
            pole * (two + one),
            back + pole * back_one,
            pole * (back_two + back_one),
        )

    zero = jnp.zeros((part, lanes), jnp.float32)
    ends = lax.fori_loop(0, rows, walk, (zero, zero, zero, zero))
    for n in range(4):
        moments[n] = ends[n]


def filter_kernel(count, where_at, freq, moments, tables, cas, out, filtered):
    rows, part, lanes = freq.shape
    slabs = moments.shape[0]
    me = where_at[0]
    pole, level, slope, decay, wrap_one, wrap_two = (tables[n] for n in range(6))

    def carried(direction, n):
        one = jnp.zeros((part, lanes), jnp.float32)
        two = one
        for m in range(slabs, 0, -1):
            other = lax.rem(me + 2 * slabs - direction * m, slabs)
            one, two = (
                decay * one + moments[other, n],
                decay * (two + rows * one) + moments[other, n + 1],
            )
        return wrap_one * one, wrap_one * two + wrap_two * one

    def forward(i, carry):
        one, two = carry
        two = pole * (two + one)
        one = freq[i] + pole * one
        filtered[i] = level * one + slope * two
        return one, two

    lax.fori_loop(0, rows, forward, carried(1, 0))

    def backward(i, carry):
        one, two = carry
        at = rows - 1 - i
        two = pole * (two + one)
        one = pole * one
        filtered[at] += level * one + slope * two
        return one + freq[at], two

    lax.fori_loop(0, rows, backward, carried(-1, 2))

    def across(g, _):
        blocks = swap_blocks([filtered[g * count + p] for p in range(count)])
        stacked = jnp.concatenate(blocks, axis=0)
        mixed = jnp.dot(cas[...], stacked, precision=HIGHEST, preferred_element_type=jnp.float32)
        for u in range(count):
            out[u, g] = mixed[u * part : (u + 1) * part]
        return 0

    lax.fori_loop(0, rows // count, across, 0)


def depth_kernel(received, cas, out):
    count, groups, part, lanes = received.shape

    def back(g, _):
        for p, plane in enumerate(swap_blocks([received[t, g] for t in range(count)])):
            out[g * count + p] = jnp.dot(
                plane, cas[...], precision=HIGHEST, preferred_element_type=jnp.float32
            )
        return 0

    lax.fori_loop(0, groups, back, 0)


def space_sum(sums):
    both = lax.psum(jnp.sum(sums, axis=(1, 2)), "space")
    return both[0], both[1]


def fast(log_k, heads, warm_adjoint, obs_columns, obs_residuals, well_columns):
    rows, width, depth = log_k.shape
    slabs = lax.axis_size("space")
    count = lax.axis_size("test")
    along = rows * slabs
    part = width // count
    block = depth // count
    first_row = lax.axis_index("space") * rows
    warm, head = warm_adjoint[0], heads[0]
    low = jnp.concatenate([log_k[:3], warm[:3], head[:1]])
    high = jnp.concatenate([log_k[rows - 3 :], warm[rows - 3 :], head[rows - 1 :]])
    before = lax.ppermute(high, "space", [(i, i + 1) for i in range(slabs - 1)])
    after = lax.ppermute(low, "space", [(i + 1, i) for i in range(slabs - 1)])
    spot = jnp.stack([first_row, jnp.int32(along), well_columns[0]]).astype(jnp.int32)
    start, image, soft, around, sums = pl.pallas_call(
        residual_kernel,
        out_shape=[
            shape(rows + 4, width, depth),
            shape(rows + 2, width, depth),
            shape(rows + 6, width, depth),
            shape(rows + 4, width, depth),
            shape(2, 8, depth),
        ],
        in_specs=[SM, SM, VM, VM, VM, VM, VM],
        out_specs=[VM] * 5,
        scratch_shapes=[pltpu.VMEM((rows + 6, width, depth), jnp.float32)],
        compiler_params=BIG,
        name="residual",
    )(spot, obs_columns, log_k, warm, before, after, obs_residuals[0])
    norm, curve = space_sum(sums)
    step = norm / curve
    sums = pl.pallas_call(
        second_kernel,
        out_shape=shape(2, 8, depth),
        in_specs=[SM, VM, VM, VM, VM],
        out_specs=VM,
        scratch_shapes=[pltpu.VMEM((rows + 2, width, depth), jnp.float32)],
        compiler_params=BIG,
        name="second",
    )(step[None], start, image, soft, around)
    norm_next, curve_next = space_sum(sums)
    ratio = norm_next / norm
    step_next = norm_next / (curve_next - ratio * norm_next / step)
    scalars = jnp.stack([step + step_next * (1.0 + ratio), step_next * step])
    cas_depth = hartley(depth)
    cas_across = hartley(width)
    sent = pl.pallas_call(
        gradient_kernel,
        out_shape=shape(count, rows // count, width, depth),
        in_specs=[SM, SM] + [VM] * 8,
        out_specs=VM,
        scratch_shapes=[pltpu.VMEM((rows + 2, width, depth), jnp.float32)] * 2,
        compiler_params=BIG,
        name="gradient",
    )(spot, scalars, warm, head, before, after, start, image, soft, cas_depth)
    summed = lax.psum_scatter(sent, "test", scatter_dimension=0)
    lanes_at = jnp.arange(depth)
    across_at = (lanes_at // block)[None, :] * part + jnp.arange(part)[:, None]
    depth_at = lax.axis_index("test") * block + lanes_at % block
    shift = 1.0 + range_squared * (
        kappa_of(across_at.astype(jnp.float32), width)
        + kappa_of(depth_at.astype(jnp.float32), depth)[None, :]
    )
    centre = 1.0 + shift / (2.0 * range_squared)
    pole = 1.0 / (centre + jnp.sqrt(centre * centre - 1.0))
    square = pole * pole
    gain = prior_gain / (range_squared * range_squared) * square / (width * depth)
    slope = gain / (1.0 - square) ** 2
    level = slope * (1.0 + square) / (1.0 - square)
    turn = pole**along
    wrap_one = 1.0 / (1.0 - turn)
    tables = jnp.stack(
        [pole, level, slope, pole**rows, wrap_one, along * turn * wrap_one * wrap_one]
    )
    freq, moments = pl.pallas_call(
        functools.partial(moment_kernel, count),
        out_shape=[shape(rows, part, depth), shape(4, part, depth)],
        in_specs=[VM] * 3,
        out_specs=[VM] * 2,
        compiler_params=BIG,
        name="moment",
    )(summed, cas_across, pole)
    moments = lax.all_gather(moments, "space")
    back = pl.pallas_call(
        functools.partial(filter_kernel, count),
        out_shape=shape(count, rows // count, part, depth),
        in_specs=[SM] + [VM] * 4,
        out_specs=VM,
        scratch_shapes=[pltpu.VMEM((rows, part, depth), jnp.float32)],
        compiler_params=BIG,
        name="filter",
    )(lax.axis_index("space").astype(jnp.int32)[None], freq, moments, tables, cas_across)
    received = lax.all_to_all(back, "test", split_axis=0, concat_axis=0, tiled=True)
    return pl.pallas_call(
        depth_kernel,
        out_shape=shape(rows, part, depth),
        in_specs=[VM] * 2,
        out_specs=VM,
        compiler_params=BIG,
        name="depth",
    )(received, cas_depth)


def pick(log_k, *rest):
    rows, width, depth = log_k.shape
    count = lax.axis_size("test")
    fits = depth == 128 and depth % count == 0 and rows % count == 0 and width % (8 * count) == 0
    return (fast if fits and rows >= 3 else on_device)(log_k, *rest)


def solution(mesh):
    placed = (
        P(("groups", "space"), None, None),
        P("test", ("groups", "space"), None, None),
        P("test", ("groups", "space"), None, None),
        P("test", "groups"),
        P("test", "groups", None),
        P(("groups", "test")),
    )
    return jax.shard_map(
        pick,
        mesh=mesh,
        in_specs=placed,
        out_specs=P(("groups", "space"), "test", None),
        check_vma=False,
    )
```

```python
import jax
import jax.numpy as jnp
from jax import lax
from jax.experimental import pallas as pl
from jax.experimental.pallas import tpu as pltpu
from jax.sharding import PartitionSpec as P

ITERS = 2


prior_gain = 5.0
range_squared = 4.0


def with_halo(cells, sides, width):
    for axis, dim in sides:
        count = lax.axis_size(axis)
        ends = count - 1
        head = lax.slice_in_dim(cells, 0, width, axis=dim)
        tail = lax.slice_in_dim(cells, cells.shape[dim] - width, cells.shape[dim], axis=dim)
        cells = jnp.concatenate(
            [
                lax.ppermute(tail, axis, [(i, (i + 1) % count) for i in range(ends)]),
                cells,
                lax.ppermute(head, axis, [((i + 1) % count, i) for i in range(ends)]),
            ],
            axis=dim,
        )
    return cells


def neighbours(padded):
    return [
        padded[2:, 1:-1, 1:-1],
        padded[:-2, 1:-1, 1:-1],
        padded[1:-1, 2:, 1:-1],
        padded[1:-1, :-2, 1:-1],
        padded[1:-1, 1:-1, 2:],
        padded[1:-1, 1:-1, :-2],
    ]


def operate(values, padded, conduct):
    summed = jnp.zeros_like(values)
    for face_k, beside in zip(conduct, neighbours(padded)):
        summed = summed + face_k * (values - beside)
    return summed


def kappa_of(indices, length):
    return 4.0 * jnp.sin(jnp.pi * indices / length) ** 2


def pad_sides(padded):
    return jnp.pad(padded, ((0, 0), (1, 1), (1, 1)))


def with_faces(values):
    return pad_sides(with_halo(values, (("space", 0),), 1))


def squares(residual):
    return lax.psum(jnp.sum(residual * residual), "space")


def hartley(length):
    indices = jnp.arange(length, dtype=jnp.int32)
    products = indices[:, None] * indices[None, :] % length
    angles = products.astype(jnp.float32) * (2.0 * jnp.pi / length)
    return jnp.cos(angles) + jnp.sin(angles)


def on_device(log_k, heads, warm_adjoint, obs_columns, obs_residuals, well_columns):
    slab_rows, width_cells, depth_cells = log_k.shape
    space_count = lax.axis_size("space")
    first_row = lax.axis_index("space") * slab_rows
    logk_pad, head_pad = (
        with_halo(log_k, (("space", 0),), 1),
        with_halo(heads[0], (("space", 0),), 1),
    )
    logk_val = log_k.astype(jnp.float32)
    conduct = [
        jnp.exp(0.5 * (logk_val + beside))
        for beside in neighbours(pad_sides(logk_pad.astype(jnp.float32)))
    ]
    columns = obs_columns[0]
    row_local = columns // width_cells - first_row
    inside = (row_local >= 0) & (row_local < slab_rows)
    row_local = jnp.where(inside, row_local, slab_rows)
    source = jnp.zeros((slab_rows, width_cells, depth_cells), jnp.float32)
    source = source.at[row_local, columns % width_cells].add(obs_residuals[0], mode="drop")
    adjoint = warm_adjoint[0].astype(jnp.float32)
    lam_padded = with_faces(adjoint)
    residual = source - operate(adjoint, lam_padded, conduct)
    direction = residual
    norm_now = squares(residual)
    for iteration in range(ITERS):
        dir_padded = with_faces(direction)
        applied = operate(direction, dir_padded, conduct)
        step_length = norm_now / lax.psum(jnp.sum(direction * applied), "space")
        adjoint = adjoint + step_length * direction
        lam_padded = lam_padded + step_length * dir_padded
        if iteration + 1 < ITERS:
            residual = residual - step_length * applied
            norm_next = squares(residual)
            direction = residual + norm_next / norm_now * direction
            norm_now = norm_next
    lam_full = pad_sides(with_halo(adjoint, (("space", 0),), 1))
    head_val = heads[0].astype(jnp.float32)
    misfit_term = jnp.zeros_like(adjoint)
    for face_k, lam_side, head_side in zip(
        conduct, neighbours(lam_full), neighbours(pad_sides(head_pad.astype(jnp.float32)))
    ):
        misfit_term = misfit_term + face_k * (adjoint - lam_side) * (head_val - head_side)
    column_ids = (first_row + jnp.arange(slab_rows, dtype=jnp.int32))[
        :, None
    ] * width_cells + jnp.arange(width_cells, dtype=jnp.int32)[None, :]
    keep_mask = (column_ids != well_columns[0]).astype(jnp.float32)
    partial_value = -0.5 * misfit_term * keep_mask[:, :, None]
    highest = lax.Precision.HIGHEST
    cas_depth = hartley(depth_cells)
    cas_across = hartley(width_cells)
    along_cells = slab_rows * space_count
    cas_along = hartley(along_cells)
    summed = lax.psum_scatter(partial_value, "test", scatter_dimension=1, tiled=True)
    depth_freq = jnp.einsum("xyz,zk->xky", summed, cas_depth, precision=highest)
    pencil = lax.all_to_all(depth_freq, "test", split_axis=1, concat_axis=2, tiled=True)
    across_freq = jnp.einsum("xzy,yk->kzx", pencil, cas_across, precision=highest)
    column_block = lax.all_to_all(across_freq, "space", split_axis=0, concat_axis=2, tiled=True)
    along_freq = jnp.einsum("yzx,xk->yzk", column_block, cas_along, precision=highest)
    across_rows = column_block.shape[0]
    depth_rows = column_block.shape[1]
    kappa_x = kappa_of(jnp.arange(along_cells).astype(jnp.float32), along_cells)
    kappa_y = kappa_of(
        (lax.axis_index("space") * across_rows + jnp.arange(across_rows)).astype(jnp.float32),
        width_cells,
    )
    kappa_z = kappa_of(
        (lax.axis_index("test") * depth_rows + jnp.arange(depth_rows)).astype(jnp.float32),
        depth_cells,
    )
    spectrum = (
        prior_gain
        / (
            1.0
            + range_squared
            * (kappa_y[:, None, None] + kappa_z[None, :, None] + kappa_x[None, None, :])
        )
        ** 2
    )
    along_back = jnp.einsum("yzk,kx->yzx", along_freq * spectrum, cas_along, precision=highest)
    slab_block = lax.all_to_all(along_back, "space", split_axis=2, concat_axis=0, tiled=True)
    across_back = jnp.einsum("yzx,yk->xzk", slab_block, cas_across, precision=highest)
    depth_block = lax.all_to_all(across_back, "test", split_axis=2, concat_axis=1, tiled=True)
    result = jnp.einsum("xky,kz->xyz", depth_block, cas_depth, precision=highest)
    scale_back = 1.0 / (along_cells * width_cells * depth_cells)
    return result * scale_back


HIGHEST = lax.Precision.HIGHEST
VM = pl.BlockSpec(memory_space=pltpu.VMEM)
SM = pl.BlockSpec(memory_space=pltpu.SMEM)
BIG = pltpu.CompilerParams(vmem_limit_bytes=60 * 1024 * 1024)


def shape(*dims, dtype=jnp.float32):
    return jax.ShapeDtypeStruct(dims, dtype)


def iotas(plane):
    return (
        lax.broadcasted_iota(jnp.int32, plane, 0),
        lax.broadcasted_iota(jnp.int32, plane, 1),
    )


def ring_sum(plane, edge):
    rows, lanes = plane.shape
    at_row, at_lane = iotas(plane.shape)
    up = jnp.where(at_row == rows - 1, edge, pltpu.roll(plane, rows - 1, 0))
    down = jnp.where(at_row == 0, edge, pltpu.roll(plane, 1, 0))
    right = jnp.where(at_lane == lanes - 1, edge, pltpu.roll(plane, lanes - 1, 1))
    left = jnp.where(at_lane == 0, edge, pltpu.roll(plane, 1, 1))
    return (up + down) + (right + left)


def plane_total(plane):
    rows, lanes = plane.shape
    return jnp.sum(plane.reshape(rows // 8, 8, lanes), axis=0)


def swap_blocks(planes):
    count = len(planes)
    lanes = planes[0].shape[1]
    block = lanes // count
    at_lane = iotas(planes[0].shape)[1] // block
    swapped = []
    for to in range(count):
        joined = planes[to]
        for frm in range(count):
            if frm != to:
                shift = (block * (frm - to)) % lanes
                joined = jnp.where(at_lane == frm, pltpu.roll(planes[frm], shift, 1), joined)
        swapped.append(joined)
    return swapped


def residual_kernel(
    spot, columns, logk, warm, before, after, observed, start, image, soft, around, sums, weighted
):
    rows, width, depth = logk.shape
    first_row, last_row = spot[0], spot[1]

    def prepare(to, logk_row, warm_row):
        soft_row = jnp.exp(0.5 * logk_row.astype(jnp.float32))
        soft[to] = soft_row
        weighted[to] = soft_row * warm_row.astype(jnp.float32)

    for i in range(3):
        prepare(i, before[i], before[3 + i])
        prepare(rows + 3 + i, after[i], after[3 + i])

    def fill(i, _):
        prepare(i + 3, logk[i], warm[i])
        return 0

    lax.fori_loop(0, rows, fill, 0)

    def first(i, _):
        row = first_row + i - 2
        inside = ((row >= 0) & (row < last_row)).astype(jnp.float32)
        soft_row = soft[i + 1]
        near = ring_sum(soft_row, 1.0) + (soft[i] + soft[i + 2])
        around[i] = near
        held = weighted[i + 1]
        beside = ring_sum(held, 0.0) + (weighted[i] + weighted[i + 2])
        start[i] = (soft_row * beside - held * near) * inside
        return 0

    lax.fori_loop(0, rows + 4, first, 0)

    def add(o, _):
        column = columns[0, o]
        row = column // width
        place = column - row * width
        local = row - first_row + 2

        @pl.when((local >= 0) & (local < rows + 4))
        def _():
            start[local, pl.ds(place, 1), :] += observed[pl.ds(o, 1), :]

        return 0

    lax.fori_loop(0, columns.shape[1], add, 0)

    def scale(i, _):
        weighted[i] = soft[i + 1] * start[i]
        return 0

    lax.fori_loop(0, rows + 4, scale, 0)

    def second(i, carry):
        total_rr, total_rq = carry
        row = first_row + i - 1
        inside = ((row >= 0) & (row < last_row)).astype(jnp.float32)
        held = weighted[i + 1]
        beside = ring_sum(held, 0.0) + (weighted[i] + weighted[i + 2])
        applied = (held * around[i + 1] - soft[i + 2] * beside) * inside
        image[i] = applied
        value = start[i + 1]
        own = ((i >= 1) & (i <= rows)).astype(jnp.float32)
        return (
            total_rr + own * plane_total(value * value),
            total_rq + own * plane_total(value * applied),
        )

    zero = jnp.zeros((8, depth), jnp.float32)
    total_rr, total_rq = lax.fori_loop(0, rows + 2, second, (zero, zero))
    sums[0] = total_rr
    sums[1] = total_rq


def second_kernel(scalars, start, image, soft, around, sums, weighted):
    rows = start.shape[0] - 4
    step = scalars[0]

    def scale(i, _):
        weighted[i] = soft[i + 2] * (start[i + 1] - step * image[i])
        return 0

    lax.fori_loop(0, rows + 2, scale, 0)

    def apply(i, carry):
        total_rr, total_rq = carry
        held = weighted[i + 1]
        beside = ring_sum(held, 0.0) + (weighted[i] + weighted[i + 2])
        value = start[i + 2] - step * image[i + 1]
        applied = held * around[i + 2] - soft[i + 3] * beside
        return total_rr + plane_total(value * value), total_rq + plane_total(value * applied)

    zero = jnp.zeros((8, start.shape[2]), jnp.float32)
    total_rr, total_rq = lax.fori_loop(0, rows, apply, (zero, zero))
    sums[0] = total_rr
    sums[1] = total_rq


def face_terms(soft, field, head, axis):
    size = soft.shape[axis]
    at = iotas(soft.shape)[axis]
    both = field * head
    ahead = size - 1
    product = (field - pltpu.roll(field, ahead, axis)) * (head - pltpu.roll(head, ahead, axis))
    upper = jnp.where(at == size - 1, both, pltpu.roll(soft, ahead, axis) * product)
    lower = jnp.where(at == 0, both, pltpu.roll(soft * product, 1, axis))
    return upper + lower


MESH = pl.DeviceIdType.MESH


def greet(others):
    barrier = pltpu.get_barrier_semaphore()
    for other in others:
        pl.semaphore_signal(barrier, inc=1, device_id=other, device_id_type=MESH)
    pl.semaphore_wait(barrier, len(others))


def gradient_kernel(
    spot,
    scalars,
    warm,
    heads,
    before,
    after,
    start,
    image,
    soft,
    cas,
    out,
    field,
    head,
    mine,
    from_mate,
    from_across,
    send_mate,
    take_mate,
    send_across,
    take_across,
):
    rows, width, depth = warm.shape
    here = lax.axis_index("test")
    half, core = here // 2, lax.rem(here, 2)
    mate = {"test": 2 * half + 1 - core}
    across = {"test": 2 * (1 - half) + core}
    greet([mate, across])
    first_row = spot[0]
    well = spot[2]
    with_start, with_image = scalars[0], scalars[1]

    def fill(to, warm_row, head_row):
        field[to] = (
            warm_row.astype(jnp.float32) + with_start * start[to + 1] - with_image * image[to]
        )
        head[to] = head_row

    fill(0, before[5], before[6])
    fill(rows + 1, after[3], after[6])

    def middle(i, _):
        fill(i + 1, warm[i], heads[i])
        return 0

    lax.fori_loop(0, rows, middle, 0)
    at_row = iotas((width, depth))[0]
    count = 4
    groups = rows // count

    def term(i):
        s, f, h = soft[i + 3], field[i + 1], head[i + 1].astype(jnp.float32)
        gathered = face_terms(s, f, h, 0) + face_terms(s, f, h, 1)
        gathered += soft[i + 2] * ((f - field[i]) * (h - head[i].astype(jnp.float32)))
        gathered += soft[i + 4] * ((f - field[i + 2]) * (h - head[i + 2].astype(jnp.float32)))
        keep = at_row != well - (first_row + i) * width
        value = jnp.where(keep, -0.5 * s * gathered, 0.0)
        return jnp.dot(value, cas[...], precision=HIGHEST, preferred_element_type=jnp.float32)

    def to_mate(g):
        return pltpu.make_async_remote_copy(
            src_ref=mine.at[1 - core, g],
            dst_ref=from_mate.at[g],
            send_sem=send_mate.at[g],
            recv_sem=take_mate.at[g],
            device_id=mate,
            device_id_type=MESH,
        )

    def to_across(g):
        return pltpu.make_async_remote_copy(
            src_ref=mine.at[core, g, 1 - half],
            dst_ref=from_across.at[g],
            send_sem=send_across.at[g],
            recv_sem=take_across.at[g],
            device_id=across,
            device_id_type=MESH,
        )

    def group(g):
        for t, plane in enumerate(swap_blocks([term(g * count + p) for p in range(count)])):
            mine[t % 2, g, t // 2] = plane
        to_mate(g).start()

    def relay(g):
        to_mate(g).wait_recv()
        mine[core, g, 1 - half] += from_mate[g, 1 - half]
        to_across(g).start()

    group(0)

    def step(g, _):
        group(g)
        relay(g - 1)
        return 0

    lax.fori_loop(1, groups, step, 0)
    relay(groups - 1)

    def finish(g, _):
        to_across(g).wait_recv()
        out[g] = (mine[core, g, half] + from_mate[g, half]) + from_across[g]
        to_mate(g).wait_send()
        to_across(g).wait_send()
        return 0

    lax.fori_loop(0, groups, finish, 0)


def spectral_kernel(
    summed,
    tables,
    cas_across,
    cas_depth,
    out,
    freq,
    moments,
    filtered,
    going,
    coming,
    send_end,
    take_end,
    send_back,
    take_back,
):
    groups, width, lanes = summed.shape
    count, part = going.shape[0], going.shape[2]
    rows = groups * count
    slabs = moments.shape[0]
    slab, here = lax.axis_index("space"), lax.axis_index("test")
    others = [{"space": lax.rem(slab + k, slabs)} for k in range(1, slabs)]
    peers = [lax.rem(here + k, count) for k in range(1, count)]
    greet(others + [{"test": peer} for peer in peers])

    def mix(g, _):
        mixed = jnp.dot(
            cas_across[...], summed[g], precision=HIGHEST, preferred_element_type=jnp.float32
        )
        blocks = [mixed[j * part : (j + 1) * part] for j in range(count)]
        for p, plane in enumerate(swap_blocks(blocks)):
            freq[g * count + p] = plane
        return 0

    lax.fori_loop(0, groups, mix, 0)
    pole, level, slope, decay, wrap_one, wrap_two = (tables[n] for n in range(6))

    def walk(i, carry):
        one, two, back_one, back_two = carry
        value, back = freq[i], freq[rows - 1 - i]
        return (
            value + pole * one,
            pole * (two + one),
            back + pole * back_one,
            pole * (back_two + back_one),
        )

    zero = jnp.zeros((part, lanes), jnp.float32)
    ends = lax.fori_loop(0, rows, walk, (zero, zero, zero, zero))
    for n in range(4):
        moments[slab, n] = ends[n]
    copies = [
        pltpu.make_async_remote_copy(
            src_ref=moments.at[slab],
            dst_ref=moments.at[slab],
            send_sem=send_end.at[k],
            recv_sem=take_end.at[k],
            device_id=other,
            device_id_type=MESH,
        )
        for k, other in enumerate(others)
    ]
    for copy in copies:
        copy.start()
    for copy in copies:
        copy.wait()

    def carried(direction, n):
        one, two = zero, zero
        for m in range(slabs, 0, -1):
            other = lax.rem(slab + 2 * slabs - direction * m, slabs)
            one, two = (
                decay * one + moments[other, n],
                decay * (two + rows * one) + moments[other, n + 1],
            )
        return wrap_one * one, wrap_one * two + wrap_two * one

    def forward(i, carry):
        one, two = carry
        two = pole * (two + one)
        one = freq[i] + pole * one
        filtered[i] = level * one + slope * two
        return one, two

    lax.fori_loop(0, rows, forward, carried(1, 0))

    def backward(i, carry):
        one, two = carry
        at = rows - 1 - i
        two = pole * (two + one)
        one = pole * one
        filtered[at] += level * one + slope * two
        return one + freq[at], two

    lax.fori_loop(0, rows, backward, carried(-1, 2))

    def to_peer(k, g):
        return pltpu.make_async_remote_copy(
            src_ref=going.at[peers[k], g],
            dst_ref=coming.at[here, g],
            send_sem=send_back.at[k, g],
            recv_sem=take_back.at[k, g],
            device_id={"test": peers[k]},
            device_id_type=MESH,
        )

    def unmix(g, _):
        blocks = swap_blocks([filtered[g * count + p] for p in range(count)])
        stacked = jnp.concatenate(blocks, axis=0)
        mixed = jnp.dot(
            cas_across[...], stacked, precision=HIGHEST, preferred_element_type=jnp.float32
        )
        for u in range(count):
            going[u, g] = mixed[u * part : (u + 1) * part]
        for k in range(count - 1):
            to_peer(k, g).start()
        coming[here, g] = going[here, g]
        return 0

    lax.fori_loop(0, groups, unmix, 0)

    def back(g, _):
        for k in range(count - 1):
            to_peer(k, g).wait()
        for p, plane in enumerate(swap_blocks([coming[t, g] for t in range(count)])):
            out[g * count + p] = jnp.dot(
                plane, cas_depth[...], precision=HIGHEST, preferred_element_type=jnp.float32
            )
        return 0

    lax.fori_loop(0, groups, back, 0)


def space_sum(sums):
    both = lax.psum(jnp.sum(sums, axis=(1, 2)), "space")
    return both[0], both[1]


def fast(log_k, heads, warm_adjoint, obs_columns, obs_residuals, well_columns):
    rows, width, depth = log_k.shape
    slabs = lax.axis_size("space")
    count = lax.axis_size("test")
    along = rows * slabs
    part = width // count
    block = depth // count
    first_row = lax.axis_index("space") * rows
    warm, head = warm_adjoint[0], heads[0]
    low = jnp.concatenate([log_k[:3], warm[:3], head[:1]])
    high = jnp.concatenate([log_k[rows - 3 :], warm[rows - 3 :], head[rows - 1 :]])
    before = lax.ppermute(high, "space", [(i, i + 1) for i in range(slabs - 1)])
    after = lax.ppermute(low, "space", [(i + 1, i) for i in range(slabs - 1)])
    spot = jnp.stack([first_row, jnp.int32(along), well_columns[0]]).astype(jnp.int32)
    start, image, soft, around, sums = pl.pallas_call(
        residual_kernel,
        out_shape=[
            shape(rows + 4, width, depth),
            shape(rows + 2, width, depth),
            shape(rows + 6, width, depth),
            shape(rows + 4, width, depth),
            shape(2, 8, depth),
        ],
        in_specs=[SM, SM, VM, VM, VM, VM, VM],
        out_specs=[VM] * 5,
        scratch_shapes=[pltpu.VMEM((rows + 6, width, depth), jnp.float32)],
        compiler_params=BIG,
        name="residual",
    )(spot, obs_columns, log_k, warm, before, after, obs_residuals[0])
    norm, curve = space_sum(sums)
    step = norm / curve
    sums = pl.pallas_call(
        second_kernel,
        out_shape=shape(2, 8, depth),
        in_specs=[SM, VM, VM, VM, VM],
        out_specs=VM,
        scratch_shapes=[pltpu.VMEM((rows + 2, width, depth), jnp.float32)],
        compiler_params=BIG,
        name="second",
    )(step[None], start, image, soft, around)
    norm_next, curve_next = space_sum(sums)
    ratio = norm_next / norm
    step_next = norm_next / (curve_next - ratio * norm_next / step)
    scalars = jnp.stack([step + step_next * (1.0 + ratio), step_next * step])
    cas_depth = hartley(depth)
    cas_across = hartley(width)
    groups = rows // count
    summed = pl.pallas_call(
        gradient_kernel,
        out_shape=shape(groups, width, depth),
        in_specs=[SM, SM] + [VM] * 8,
        out_specs=VM,
        scratch_shapes=[
            pltpu.VMEM((rows + 2, width, depth), jnp.float32),
            pltpu.VMEM((rows + 2, width, depth), jnp.bfloat16),
            pltpu.VMEM((2, groups, 2, width, depth), jnp.float32),
            pltpu.VMEM((groups, 2, width, depth), jnp.float32),
            pltpu.VMEM((groups, width, depth), jnp.float32),
        ]
        + [pltpu.SemaphoreType.DMA((groups,))] * 4,
        compiler_params=pltpu.CompilerParams(
            vmem_limit_bytes=60 * 1024 * 1024, collective_id=1, has_side_effects=True
        ),
        name="gradient",
    )(spot, scalars, warm, head, before, after, start, image, soft, cas_depth)
    lanes_at = jnp.arange(depth)
    across_at = (lanes_at // block)[None, :] * part + jnp.arange(part)[:, None]
    depth_at = lax.axis_index("test") * block + lanes_at % block
    shift = 1.0 + range_squared * (
        kappa_of(across_at.astype(jnp.float32), width)
        + kappa_of(depth_at.astype(jnp.float32), depth)[None, :]
    )
    centre = 1.0 + shift / (2.0 * range_squared)
    pole = 1.0 / (centre + jnp.sqrt(centre * centre - 1.0))
    square = pole * pole
    gain = prior_gain / (range_squared * range_squared) * square / (width * depth)
    slope = gain / (1.0 - square) ** 2
    level = slope * (1.0 + square) / (1.0 - square)
    turn = pole**along
    wrap_one = 1.0 / (1.0 - turn)
    tables = jnp.stack(
        [pole, level, slope, pole**rows, wrap_one, along * turn * wrap_one * wrap_one]
    )
    return pl.pallas_call(
        spectral_kernel,
        out_shape=shape(rows, part, depth),
        in_specs=[VM] * 4,
        out_specs=VM,
        scratch_shapes=[
            pltpu.VMEM((rows, part, depth), jnp.float32),
            pltpu.VMEM((slabs, 4, part, depth), jnp.float32),
            pltpu.VMEM((rows, part, depth), jnp.float32),
            pltpu.VMEM((count, groups, part, depth), jnp.float32),
            pltpu.VMEM((count, groups, part, depth), jnp.float32),
            pltpu.SemaphoreType.DMA((slabs - 1,)),
            pltpu.SemaphoreType.DMA((slabs - 1,)),
            pltpu.SemaphoreType.DMA((count - 1, groups)),
            pltpu.SemaphoreType.DMA((count - 1, groups)),
        ],
        compiler_params=pltpu.CompilerParams(
            vmem_limit_bytes=40 * 1024 * 1024, collective_id=2, has_side_effects=True
        ),
        name="spectral",
    )(summed, tables, cas_across, cas_depth)


def pick(log_k, *rest):
    rows, width, depth = log_k.shape
    count = lax.axis_size("test")
    fits = depth == 128 and count == 4 and rows % count == 0 and width % (8 * count) == 0
    return (fast if fits and lax.axis_size("space") > 1 else on_device)(log_k, *rest)


def solution(mesh):
    placed = (
        P(("groups", "space"), None, None),
        P("test", ("groups", "space"), None, None),
        P("test", ("groups", "space"), None, None),
        P("test", "groups"),
        P("test", "groups", None),
        P(("groups", "test")),
    )
    return jax.shard_map(
        pick,
        mesh=mesh,
        in_specs=placed,
        out_specs=P(("groups", "space"), "test", None),
        check_vma=False,
    )
```

```python
import jax
import jax.numpy as jnp
import numpy as np
from jax import lax
from jax.experimental import pallas as pl
from jax.experimental.pallas import tpu as pltpu
from jax.sharding import PartitionSpec as P

ITERS = 2


prior_gain = 5.0
range_squared = 4.0


def with_halo(cells, sides, width):
    for axis, dim in sides:
        count = lax.axis_size(axis)
        ends = count - 1
        head = lax.slice_in_dim(cells, 0, width, axis=dim)
        tail = lax.slice_in_dim(cells, cells.shape[dim] - width, cells.shape[dim], axis=dim)
        cells = jnp.concatenate(
            [
                lax.ppermute(tail, axis, [(i, (i + 1) % count) for i in range(ends)]),
                cells,
                lax.ppermute(head, axis, [((i + 1) % count, i) for i in range(ends)]),
            ],
            axis=dim,
        )
    return cells


def neighbours(padded):
    return [
        padded[2:, 1:-1, 1:-1],
        padded[:-2, 1:-1, 1:-1],
        padded[1:-1, 2:, 1:-1],
        padded[1:-1, :-2, 1:-1],
        padded[1:-1, 1:-1, 2:],
        padded[1:-1, 1:-1, :-2],
    ]


def operate(values, padded, conduct):
    summed = jnp.zeros_like(values)
    for face_k, beside in zip(conduct, neighbours(padded)):
        summed = summed + face_k * (values - beside)
    return summed


def kappa_of(indices, length):
    return 4.0 * jnp.sin(jnp.pi * indices / length) ** 2


def pad_sides(padded):
    return jnp.pad(padded, ((0, 0), (1, 1), (1, 1)))


def with_faces(values):
    return pad_sides(with_halo(values, (("space", 0),), 1))


def squares(residual):
    return lax.psum(jnp.sum(residual * residual), "space")


def hartley(length):
    indices = jnp.arange(length, dtype=jnp.int32)
    products = indices[:, None] * indices[None, :] % length
    angles = products.astype(jnp.float32) * (2.0 * jnp.pi / length)
    return jnp.cos(angles) + jnp.sin(angles)


def on_device(log_k, heads, warm_adjoint, obs_columns, obs_residuals, well_columns):
    slab_rows, width_cells, depth_cells = log_k.shape
    space_count = lax.axis_size("space")
    first_row = lax.axis_index("space") * slab_rows
    logk_pad, head_pad = (
        with_halo(log_k, (("space", 0),), 1),
        with_halo(heads[0], (("space", 0),), 1),
    )
    logk_val = log_k.astype(jnp.float32)
    conduct = [
        jnp.exp(0.5 * (logk_val + beside))
        for beside in neighbours(pad_sides(logk_pad.astype(jnp.float32)))
    ]
    columns = obs_columns[0]
    row_local = columns // width_cells - first_row
    inside = (row_local >= 0) & (row_local < slab_rows)
    row_local = jnp.where(inside, row_local, slab_rows)
    source = jnp.zeros((slab_rows, width_cells, depth_cells), jnp.float32)
    source = source.at[row_local, columns % width_cells].add(obs_residuals[0], mode="drop")
    adjoint = warm_adjoint[0].astype(jnp.float32)
    lam_padded = with_faces(adjoint)
    residual = source - operate(adjoint, lam_padded, conduct)
    direction = residual
    norm_now = squares(residual)
    for iteration in range(ITERS):
        dir_padded = with_faces(direction)
        applied = operate(direction, dir_padded, conduct)
        step_length = norm_now / lax.psum(jnp.sum(direction * applied), "space")
        adjoint = adjoint + step_length * direction
        lam_padded = lam_padded + step_length * dir_padded
        if iteration + 1 < ITERS:
            residual = residual - step_length * applied
            norm_next = squares(residual)
            direction = residual + norm_next / norm_now * direction
            norm_now = norm_next
    lam_full = pad_sides(with_halo(adjoint, (("space", 0),), 1))
    head_val = heads[0].astype(jnp.float32)
    misfit_term = jnp.zeros_like(adjoint)
    for face_k, lam_side, head_side in zip(
        conduct, neighbours(lam_full), neighbours(pad_sides(head_pad.astype(jnp.float32)))
    ):
        misfit_term = misfit_term + face_k * (adjoint - lam_side) * (head_val - head_side)
    column_ids = (first_row + jnp.arange(slab_rows, dtype=jnp.int32))[
        :, None
    ] * width_cells + jnp.arange(width_cells, dtype=jnp.int32)[None, :]
    keep_mask = (column_ids != well_columns[0]).astype(jnp.float32)
    partial_value = -0.5 * misfit_term * keep_mask[:, :, None]
    highest = lax.Precision.HIGHEST
    cas_depth = hartley(depth_cells)
    cas_across = hartley(width_cells)
    along_cells = slab_rows * space_count
    cas_along = hartley(along_cells)
    summed = lax.psum_scatter(partial_value, "test", scatter_dimension=1, tiled=True)
    depth_freq = jnp.einsum("xyz,zk->xky", summed, cas_depth, precision=highest)
    pencil = lax.all_to_all(depth_freq, "test", split_axis=1, concat_axis=2, tiled=True)
    across_freq = jnp.einsum("xzy,yk->kzx", pencil, cas_across, precision=highest)
    column_block = lax.all_to_all(across_freq, "space", split_axis=0, concat_axis=2, tiled=True)
    along_freq = jnp.einsum("yzx,xk->yzk", column_block, cas_along, precision=highest)
    across_rows = column_block.shape[0]
    depth_rows = column_block.shape[1]
    kappa_x = kappa_of(jnp.arange(along_cells).astype(jnp.float32), along_cells)
    kappa_y = kappa_of(
        (lax.axis_index("space") * across_rows + jnp.arange(across_rows)).astype(jnp.float32),
        width_cells,
    )
    kappa_z = kappa_of(
        (lax.axis_index("test") * depth_rows + jnp.arange(depth_rows)).astype(jnp.float32),
        depth_cells,
    )
    spectrum = (
        prior_gain
        / (
            1.0
            + range_squared
            * (kappa_y[:, None, None] + kappa_z[None, :, None] + kappa_x[None, None, :])
        )
        ** 2
    )
    along_back = jnp.einsum("yzk,kx->yzx", along_freq * spectrum, cas_along, precision=highest)
    slab_block = lax.all_to_all(along_back, "space", split_axis=2, concat_axis=0, tiled=True)
    across_back = jnp.einsum("yzx,yk->xzk", slab_block, cas_across, precision=highest)
    depth_block = lax.all_to_all(across_back, "test", split_axis=2, concat_axis=1, tiled=True)
    result = jnp.einsum("xky,kz->xyz", depth_block, cas_depth, precision=highest)
    scale_back = 1.0 / (along_cells * width_cells * depth_cells)
    return result * scale_back


HIGHEST = lax.Precision.HIGHEST
VM = pl.BlockSpec(memory_space=pltpu.VMEM)
SM = pl.BlockSpec(memory_space=pltpu.SMEM)
BIG = pltpu.CompilerParams(vmem_limit_bytes=60 * 1024 * 1024)


def shape(*dims, dtype=jnp.float32):
    return jax.ShapeDtypeStruct(dims, dtype)


def iotas(plane):
    return (
        lax.broadcasted_iota(jnp.int32, plane, 0),
        lax.broadcasted_iota(jnp.int32, plane, 1),
    )


def ring_sum(plane, edge):
    rows, lanes = plane.shape
    at_row, at_lane = iotas(plane.shape)
    up = jnp.where(at_row == rows - 1, edge, pltpu.roll(plane, rows - 1, 0))
    down = jnp.where(at_row == 0, edge, pltpu.roll(plane, 1, 0))
    right = jnp.where(at_lane == lanes - 1, edge, pltpu.roll(plane, lanes - 1, 1))
    left = jnp.where(at_lane == 0, edge, pltpu.roll(plane, 1, 1))
    return (up + down) + (right + left)


def plane_total(plane):
    rows, lanes = plane.shape
    return jnp.sum(plane.reshape(rows // 8, 8, lanes), axis=0)


def swap_blocks(planes):
    count = len(planes)
    lanes = planes[0].shape[1]
    block = lanes // count
    at_lane = iotas(planes[0].shape)[1] // block
    swapped = []
    for to in range(count):
        joined = planes[to]
        for frm in range(count):
            if frm != to:
                shift = (block * (frm - to)) % lanes
                joined = jnp.where(at_lane == frm, pltpu.roll(planes[frm], shift, 1), joined)
        swapped.append(joined)
    return swapped


def residual_kernel(
    spot, columns, logk, warm, before, after, observed, start, image, soft, sums, weighted, around
):
    rows, width, depth = logk.shape
    first_row, last_row = spot[0], spot[1]

    def prepare(to, logk_row, warm_row):
        soft_row = jnp.exp(0.5 * logk_row.astype(jnp.float32))
        soft[to] = soft_row
        weighted[to] = soft_row * warm_row.astype(jnp.float32)

    for i in range(3):
        prepare(i, before[i], before[3 + i])
        prepare(rows + 3 + i, after[i], after[3 + i])

    def fill(i, _):
        prepare(i + 3, logk[i], warm[i])
        return 0

    lax.fori_loop(0, rows, fill, 0)

    def first(i, _):
        row = first_row + i - 2
        inside = ((row >= 0) & (row < last_row)).astype(jnp.float32)
        soft_row = soft[i + 1]
        near = ring_sum(soft_row, 1.0) + (soft[i] + soft[i + 2])
        around[i] = near
        held = weighted[i + 1]
        beside = ring_sum(held, 0.0) + (weighted[i] + weighted[i + 2])
        start[i] = (soft_row * beside - held * near) * inside
        return 0

    lax.fori_loop(0, rows + 4, first, 0)

    def add(o, _):
        column = columns[0, o]
        row = column // width
        place = column - row * width
        local = row - first_row + 2

        @pl.when((local >= 0) & (local < rows + 4))
        def _():
            start[local, pl.ds(place, 1), :] += observed[pl.ds(o, 1), :]

        return 0

    lax.fori_loop(0, columns.shape[1], add, 0)

    def scale(i, _):
        weighted[i] = soft[i + 1] * start[i]
        return 0

    lax.fori_loop(0, rows + 4, scale, 0)

    def second(i, carry):
        total_rr, total_rq = carry
        row = first_row + i - 1
        inside = ((row >= 0) & (row < last_row)).astype(jnp.float32)
        held = weighted[i + 1]
        beside = ring_sum(held, 0.0) + (weighted[i] + weighted[i + 2])
        applied = (held * around[i + 1] - soft[i + 2] * beside) * inside
        image[i] = applied
        value = start[i + 1]
        own = ((i >= 1) & (i <= rows)).astype(jnp.float32)
        return (
            total_rr + own * plane_total(value * value),
            total_rq + own * plane_total(value * applied),
        )

    zero = jnp.zeros((8, depth), jnp.float32)
    total_rr, total_rq = lax.fori_loop(0, rows + 2, second, (zero, zero))
    sums[0] = total_rr
    sums[1] = total_rq


def face_terms(soft, field, head, axis):
    size = soft.shape[axis]
    at = iotas(soft.shape)[axis]
    both = field * head
    ahead = size - 1
    product = (field - pltpu.roll(field, ahead, axis)) * (head - pltpu.roll(head, ahead, axis))
    upper = jnp.where(at == size - 1, both, pltpu.roll(soft, ahead, axis) * product)
    lower = jnp.where(at == 0, both, pltpu.roll(soft * product, 1, axis))
    return upper + lower


MESH = pl.DeviceIdType.MESH


def greet(others):
    barrier = pltpu.get_barrier_semaphore()
    for other in others:
        pl.semaphore_signal(barrier, inc=1, device_id=other, device_id_type=MESH)
    pl.semaphore_wait(barrier, len(others))


def gradient_kernel(
    spot,
    sums,
    warm,
    heads,
    before,
    after,
    start,
    image,
    soft,
    cas,
    out,
    field,
    head,
    mine,
    from_mate,
    from_across,
    send_mate,
    take_mate,
    send_across,
    take_across,
    shared,
    send_sum,
    take_sum,
):
    rows, width, depth = warm.shape
    slabs = shared.shape[1]
    slab = lax.axis_index("space")
    others = [{"space": lax.rem(slab + k, slabs)} for k in range(1, slabs)]
    here = lax.axis_index("test")
    half, core = here // 2, lax.rem(here, 2)
    mate = {"test": 2 * half + 1 - core}
    across = {"test": 2 * (1 - half) + core}
    greet(others + [mate, across])
    first_row = spot[0]
    well = spot[2]

    def share(turn):
        return [
            pltpu.make_async_remote_copy(
                src_ref=shared.at[turn, slab],
                dst_ref=shared.at[turn, slab],
                send_sem=send_sum.at[turn, k],
                recv_sem=take_sum.at[turn, k],
                device_id=other,
                device_id_type=MESH,
            )
            for k, other in enumerate(others)
        ]

    def gathered_sum(turn, n):
        total = shared[turn, 0, n]
        for m in range(1, slabs):
            total = total + shared[turn, m, n]
        return jnp.broadcast_to(jnp.sum(total, axis=(0, 1), keepdims=True), (1, depth))

    shared[0, slab] = sums[...]
    for copy in share(0):
        copy.start()
    head[0] = before[6]
    head[rows + 1] = after[6]

    def keep_head(i, _):
        head[i + 1] = heads[i]
        return 0

    lax.fori_loop(0, rows, keep_head, 0)
    for copy in share(0):
        copy.wait()
    norm, curve = gathered_sum(0, 0), gathered_sum(0, 1)
    length = norm / curve

    def scale(i, _):
        field[i] = soft[i + 2] * (start[i + 1] - length * image[i])
        return 0

    lax.fori_loop(0, rows + 2, scale, 0)

    def apply(i, carry):
        total_rr, total_rq = carry
        held = field[i + 1]
        beside = ring_sum(held, 0.0) + (field[i] + field[i + 2])
        near = ring_sum(soft[i + 3], 1.0) + (soft[i + 2] + soft[i + 4])
        value = start[i + 2] - length * image[i + 1]
        applied = held * near - soft[i + 3] * beside
        return total_rr + plane_total(value * value), total_rq + plane_total(value * applied)

    zero = jnp.zeros((8, depth), jnp.float32)
    total_rr, total_rq = lax.fori_loop(0, rows, apply, (zero, zero))
    shared[1, slab, 0] = total_rr
    shared[1, slab, 1] = total_rq
    for copy in share(1):
        copy.start()
    for copy in share(1):
        copy.wait()
    norm_next, curve_next = gathered_sum(1, 0), gathered_sum(1, 1)
    ratio = norm_next / norm
    length_next = norm_next / (curve_next - ratio * norm_next / length)
    with_start = length + length_next * (1.0 + ratio)
    with_image = length_next * length

    def fill(to, warm_row):
        field[to] = (
            warm_row.astype(jnp.float32) + with_start * start[to + 1] - with_image * image[to]
        )

    fill(0, before[5])
    fill(rows + 1, after[3])

    def middle(i, _):
        fill(i + 1, warm[i])
        return 0

    lax.fori_loop(0, rows, middle, 0)
    at_row = iotas((width, depth))[0]
    count = 4
    groups = rows // count

    def term(i):
        s, f, h = soft[i + 3], field[i + 1], head[i + 1].astype(jnp.float32)
        gathered = face_terms(s, f, h, 0) + face_terms(s, f, h, 1)
        gathered += soft[i + 2] * ((f - field[i]) * (h - head[i].astype(jnp.float32)))
        gathered += soft[i + 4] * ((f - field[i + 2]) * (h - head[i + 2].astype(jnp.float32)))
        keep = at_row != well - (first_row + i) * width
        value = jnp.where(keep, -0.5 * s * gathered, 0.0)
        return jnp.dot(value, cas[...], precision=HIGHEST, preferred_element_type=jnp.float32)

    def to_mate(g):
        return pltpu.make_async_remote_copy(
            src_ref=mine.at[1 - core, g],
            dst_ref=from_mate.at[g],
            send_sem=send_mate.at[g],
            recv_sem=take_mate.at[g],
            device_id=mate,
            device_id_type=MESH,
        )

    def to_across(g):
        return pltpu.make_async_remote_copy(
            src_ref=mine.at[core, g, 1 - half],
            dst_ref=from_across.at[g],
            send_sem=send_across.at[g],
            recv_sem=take_across.at[g],
            device_id=across,
            device_id_type=MESH,
        )

    def group(g):
        for t, plane in enumerate(swap_blocks([term(g * count + p) for p in range(count)])):
            mine[t % 2, g, t // 2] = plane
        to_mate(g).start()

    def relay(g):
        to_mate(g).wait_recv()
        mine[core, g, 1 - half] += from_mate[g, 1 - half]
        to_across(g).start()

    group(0)

    def step(g, _):
        group(g)
        relay(g - 1)
        return 0

    lax.fori_loop(1, groups, step, 0)
    relay(groups - 1)

    def finish(g, _):
        to_across(g).wait_recv()
        out[g] = (mine[core, g, half] + from_mate[g, half]) + from_across[g]
        to_mate(g).wait_send()
        to_across(g).wait_send()
        return 0

    lax.fori_loop(0, groups, finish, 0)


def spectral_kernel(
    summed,
    tables,
    cas_across,
    cas_depth,
    out,
    freq,
    moments,
    filtered,
    going,
    coming,
    send_end,
    take_end,
    send_back,
    take_back,
):
    groups, width, lanes = summed.shape
    count, part = going.shape[0], going.shape[2]
    rows = groups * count
    slabs = moments.shape[0]
    slab, here = lax.axis_index("space"), lax.axis_index("test")
    others = [{"space": lax.rem(slab + k, slabs)} for k in range(1, slabs)]
    peers = [lax.rem(here + k, count) for k in range(1, count)]
    greet(others + [{"test": peer} for peer in peers])

    def mix(g, _):
        mixed = jnp.dot(
            cas_across[...], summed[g], precision=HIGHEST, preferred_element_type=jnp.float32
        )
        blocks = [mixed[j * part : (j + 1) * part] for j in range(count)]
        for p, plane in enumerate(swap_blocks(blocks)):
            freq[g * count + p] = plane
        return 0

    lax.fori_loop(0, groups, mix, 0)
    pole, level, slope, decay, wrap_one, wrap_two = (tables[n] for n in range(6))

    def walk(i, carry):
        one, two, back_one, back_two = carry
        value, back = freq[i], freq[rows - 1 - i]
        return (
            value + pole * one,
            pole * (two + one),
            back + pole * back_one,
            pole * (back_two + back_one),
        )

    zero = jnp.zeros((part, lanes), jnp.float32)
    ends = lax.fori_loop(0, rows, walk, (zero, zero, zero, zero))
    for n in range(4):
        moments[slab, n] = ends[n]
    copies = [
        pltpu.make_async_remote_copy(
            src_ref=moments.at[slab],
            dst_ref=moments.at[slab],
            send_sem=send_end.at[k],
            recv_sem=take_end.at[k],
            device_id=other,
            device_id_type=MESH,
        )
        for k, other in enumerate(others)
    ]
    for copy in copies:
        copy.start()
    for copy in copies:
        copy.wait()

    def carried(direction, n):
        one, two = zero, zero
        for m in range(slabs, 0, -1):
            other = lax.rem(slab + 2 * slabs - direction * m, slabs)
            one, two = (
                decay * one + moments[other, n],
                decay * (two + rows * one) + moments[other, n + 1],
            )
        return wrap_one * one, wrap_one * two + wrap_two * one

    def forward(i, carry):
        one, two = carry
        two = pole * (two + one)
        one = freq[i] + pole * one
        filtered[i] = level * one + slope * two
        return one, two

    lax.fori_loop(0, rows, forward, carried(1, 0))

    def backward(i, carry):
        one, two = carry
        at = rows - 1 - i
        two = pole * (two + one)
        one = pole * one
        filtered[at] += level * one + slope * two
        return one + freq[at], two

    lax.fori_loop(0, rows, backward, carried(-1, 2))

    def to_peer(k, g):
        return pltpu.make_async_remote_copy(
            src_ref=going.at[peers[k], g],
            dst_ref=coming.at[here, g],
            send_sem=send_back.at[k, g],
            recv_sem=take_back.at[k, g],
            device_id={"test": peers[k]},
            device_id_type=MESH,
        )

    def unmix(g, _):
        blocks = swap_blocks([filtered[g * count + p] for p in range(count)])
        stacked = jnp.concatenate(blocks, axis=0)
        mixed = jnp.dot(
            cas_across[...], stacked, precision=HIGHEST, preferred_element_type=jnp.float32
        )
        for u in range(count):
            going[u, g] = mixed[u * part : (u + 1) * part]
        for k in range(count - 1):
            to_peer(k, g).start()
        coming[here, g] = going[here, g]
        return 0

    lax.fori_loop(0, groups, unmix, 0)

    def back(g, _):
        for k in range(count - 1):
            to_peer(k, g).wait()
        for p, plane in enumerate(swap_blocks([coming[t, g] for t in range(count)])):
            out[g * count + p] = jnp.dot(
                plane, cas_depth[...], precision=HIGHEST, preferred_element_type=jnp.float32
            )
        return 0

    lax.fori_loop(0, groups, back, 0)


def table(length):
    indices = np.arange(length)
    angles = (indices[:, None] * indices[None, :] % length) * (2.0 * np.pi / length)
    return jnp.asarray((np.cos(angles) + np.sin(angles)).astype(np.float32))


def fast(log_k, heads, warm_adjoint, obs_columns, obs_residuals, well_columns):
    rows, width, depth = log_k.shape
    slabs = lax.axis_size("space")
    count = lax.axis_size("test")
    along = rows * slabs
    part = width // count
    block = depth // count
    first_row = lax.axis_index("space") * rows
    warm, head = warm_adjoint[0], heads[0]
    low = jnp.concatenate([log_k[:3], warm[:3], head[:1]])
    high = jnp.concatenate([log_k[rows - 3 :], warm[rows - 3 :], head[rows - 1 :]])
    before = lax.ppermute(high, "space", [(i, i + 1) for i in range(slabs - 1)])
    after = lax.ppermute(low, "space", [(i + 1, i) for i in range(slabs - 1)])
    spot = jnp.stack([first_row, jnp.int32(along), well_columns[0]]).astype(jnp.int32)
    start, image, soft, sums = pl.pallas_call(
        residual_kernel,
        out_shape=[
            shape(rows + 4, width, depth),
            shape(rows + 2, width, depth),
            shape(rows + 6, width, depth),
            shape(2, 8, depth),
        ],
        in_specs=[SM, SM, VM, VM, VM, VM, VM],
        out_specs=[VM] * 4,
        scratch_shapes=[
            pltpu.VMEM((rows + 6, width, depth), jnp.float32),
            pltpu.VMEM((rows + 4, width, depth), jnp.float32),
        ],
        compiler_params=BIG,
        name="residual",
    )(spot, obs_columns, log_k, warm, before, after, obs_residuals[0])
    cas_depth = table(depth)
    cas_across = table(width)
    groups = rows // count
    summed = pl.pallas_call(
        gradient_kernel,
        out_shape=shape(groups, width, depth),
        in_specs=[SM] + [VM] * 9,
        out_specs=VM,
        scratch_shapes=[
            pltpu.VMEM((rows + 2, width, depth), jnp.float32),
            pltpu.VMEM((rows + 2, width, depth), jnp.bfloat16),
            pltpu.VMEM((2, groups, 2, width, depth), jnp.float32),
            pltpu.VMEM((groups, 2, width, depth), jnp.float32),
            pltpu.VMEM((groups, width, depth), jnp.float32),
        ]
        + [pltpu.SemaphoreType.DMA((groups,))] * 4
        + [pltpu.VMEM((2, slabs, 2, 8, depth), jnp.float32)]
        + [pltpu.SemaphoreType.DMA((2, slabs - 1))] * 2,
        compiler_params=pltpu.CompilerParams(
            vmem_limit_bytes=60 * 1024 * 1024, collective_id=1, has_side_effects=True
        ),
        name="gradient",
    )(spot, sums, warm, head, before, after, start, image, soft, cas_depth)
    lanes_at = jnp.arange(depth)
    across_at = (lanes_at // block)[None, :] * part + jnp.arange(part)[:, None]
    depth_at = lax.axis_index("test") * block + lanes_at % block
    shift = 1.0 + range_squared * (
        kappa_of(across_at.astype(jnp.float32), width)
        + kappa_of(depth_at.astype(jnp.float32), depth)[None, :]
    )
    centre = 1.0 + shift / (2.0 * range_squared)
    pole = 1.0 / (centre + jnp.sqrt(centre * centre - 1.0))
    square = pole * pole
    gain = prior_gain / (range_squared * range_squared) * square / (width * depth)
    slope = gain / (1.0 - square) ** 2
    level = slope * (1.0 + square) / (1.0 - square)
    turn = pole**along
    wrap_one = 1.0 / (1.0 - turn)
    tables = jnp.stack(
        [pole, level, slope, pole**rows, wrap_one, along * turn * wrap_one * wrap_one]
    )
    return pl.pallas_call(
        spectral_kernel,
        out_shape=shape(rows, part, depth),
        in_specs=[VM] * 4,
        out_specs=VM,
        scratch_shapes=[
            pltpu.VMEM((rows, part, depth), jnp.float32),
            pltpu.VMEM((slabs, 4, part, depth), jnp.float32),
            pltpu.VMEM((rows, part, depth), jnp.float32),
            pltpu.VMEM((count, groups, part, depth), jnp.float32),
            pltpu.VMEM((count, groups, part, depth), jnp.float32),
            pltpu.SemaphoreType.DMA((slabs - 1,)),
            pltpu.SemaphoreType.DMA((slabs - 1,)),
            pltpu.SemaphoreType.DMA((count - 1, groups)),
            pltpu.SemaphoreType.DMA((count - 1, groups)),
        ],
        compiler_params=pltpu.CompilerParams(
            vmem_limit_bytes=40 * 1024 * 1024, collective_id=2, has_side_effects=True
        ),
        name="spectral",
    )(summed, tables, cas_across, cas_depth)


def pick(log_k, *rest):
    rows, width, depth = log_k.shape
    count = lax.axis_size("test")
    fits = depth == 128 and count == 4 and rows % count == 0 and width % (8 * count) == 0
    return (fast if fits and lax.axis_size("space") > 1 else on_device)(log_k, *rest)


def solution(mesh):
    placed = (
        P(("groups", "space"), None, None),
        P("test", ("groups", "space"), None, None),
        P("test", ("groups", "space"), None, None),
        P("test", "groups"),
        P("test", "groups", None),
        P(("groups", "test")),
    )
    return jax.shard_map(
        pick,
        mesh=mesh,
        in_specs=placed,
        out_specs=P(("groups", "space"), "test", None),
        check_vma=False,
    )
```

```python
import jax
import jax.numpy as jnp
import numpy as np
from jax import lax
from jax.experimental import pallas as pl
from jax.experimental.pallas import tpu as pltpu
from jax.sharding import PartitionSpec as P

ITERS = 2


prior_gain = 5.0
range_squared = 4.0


def with_halo(cells, sides, width):
    for axis, dim in sides:
        count = lax.axis_size(axis)
        ends = count - 1
        head = lax.slice_in_dim(cells, 0, width, axis=dim)
        tail = lax.slice_in_dim(cells, cells.shape[dim] - width, cells.shape[dim], axis=dim)
        cells = jnp.concatenate(
            [
                lax.ppermute(tail, axis, [(i, (i + 1) % count) for i in range(ends)]),
                cells,
                lax.ppermute(head, axis, [((i + 1) % count, i) for i in range(ends)]),
            ],
            axis=dim,
        )
    return cells


def neighbours(padded):
    return [
        padded[2:, 1:-1, 1:-1],
        padded[:-2, 1:-1, 1:-1],
        padded[1:-1, 2:, 1:-1],
        padded[1:-1, :-2, 1:-1],
        padded[1:-1, 1:-1, 2:],
        padded[1:-1, 1:-1, :-2],
    ]


def operate(values, padded, conduct):
    summed = jnp.zeros_like(values)
    for face_k, beside in zip(conduct, neighbours(padded)):
        summed = summed + face_k * (values - beside)
    return summed


def kappa_of(indices, length):
    return 4.0 * jnp.sin(jnp.pi * indices / length) ** 2


def pad_sides(padded):
    return jnp.pad(padded, ((0, 0), (1, 1), (1, 1)))


def with_faces(values):
    return pad_sides(with_halo(values, (("space", 0),), 1))


def squares(residual):
    return lax.psum(jnp.sum(residual * residual), "space")


def hartley(length):
    indices = jnp.arange(length, dtype=jnp.int32)
    products = indices[:, None] * indices[None, :] % length
    angles = products.astype(jnp.float32) * (2.0 * jnp.pi / length)
    return jnp.cos(angles) + jnp.sin(angles)


def on_device(log_k, heads, warm_adjoint, obs_columns, obs_residuals, well_columns):
    slab_rows, width_cells, depth_cells = log_k.shape
    space_count = lax.axis_size("space")
    first_row = lax.axis_index("space") * slab_rows
    logk_pad, head_pad = (
        with_halo(log_k, (("space", 0),), 1),
        with_halo(heads[0], (("space", 0),), 1),
    )
    logk_val = log_k.astype(jnp.float32)
    conduct = [
        jnp.exp(0.5 * (logk_val + beside))
        for beside in neighbours(pad_sides(logk_pad.astype(jnp.float32)))
    ]
    columns = obs_columns[0]
    row_local = columns // width_cells - first_row
    inside = (row_local >= 0) & (row_local < slab_rows)
    row_local = jnp.where(inside, row_local, slab_rows)
    source = jnp.zeros((slab_rows, width_cells, depth_cells), jnp.float32)
    source = source.at[row_local, columns % width_cells].add(obs_residuals[0], mode="drop")
    adjoint = warm_adjoint[0].astype(jnp.float32)
    lam_padded = with_faces(adjoint)
    residual = source - operate(adjoint, lam_padded, conduct)
    direction = residual
    norm_now = squares(residual)
    for iteration in range(ITERS):
        dir_padded = with_faces(direction)
        applied = operate(direction, dir_padded, conduct)
        step_length = norm_now / lax.psum(jnp.sum(direction * applied), "space")
        adjoint = adjoint + step_length * direction
        lam_padded = lam_padded + step_length * dir_padded
        if iteration + 1 < ITERS:
            residual = residual - step_length * applied
            norm_next = squares(residual)
            direction = residual + norm_next / norm_now * direction
            norm_now = norm_next
    lam_full = pad_sides(with_halo(adjoint, (("space", 0),), 1))
    head_val = heads[0].astype(jnp.float32)
    misfit_term = jnp.zeros_like(adjoint)
    for face_k, lam_side, head_side in zip(
        conduct, neighbours(lam_full), neighbours(pad_sides(head_pad.astype(jnp.float32)))
    ):
        misfit_term = misfit_term + face_k * (adjoint - lam_side) * (head_val - head_side)
    column_ids = (first_row + jnp.arange(slab_rows, dtype=jnp.int32))[
        :, None
    ] * width_cells + jnp.arange(width_cells, dtype=jnp.int32)[None, :]
    keep_mask = (column_ids != well_columns[0]).astype(jnp.float32)
    partial_value = -0.5 * misfit_term * keep_mask[:, :, None]
    highest = lax.Precision.HIGHEST
    cas_depth = hartley(depth_cells)
    cas_across = hartley(width_cells)
    along_cells = slab_rows * space_count
    cas_along = hartley(along_cells)
    summed = lax.psum_scatter(partial_value, "test", scatter_dimension=1, tiled=True)
    depth_freq = jnp.einsum("xyz,zk->xky", summed, cas_depth, precision=highest)
    pencil = lax.all_to_all(depth_freq, "test", split_axis=1, concat_axis=2, tiled=True)
    across_freq = jnp.einsum("xzy,yk->kzx", pencil, cas_across, precision=highest)
    column_block = lax.all_to_all(across_freq, "space", split_axis=0, concat_axis=2, tiled=True)
    along_freq = jnp.einsum("yzx,xk->yzk", column_block, cas_along, precision=highest)
    across_rows = column_block.shape[0]
    depth_rows = column_block.shape[1]
    kappa_x = kappa_of(jnp.arange(along_cells).astype(jnp.float32), along_cells)
    kappa_y = kappa_of(
        (lax.axis_index("space") * across_rows + jnp.arange(across_rows)).astype(jnp.float32),
        width_cells,
    )
    kappa_z = kappa_of(
        (lax.axis_index("test") * depth_rows + jnp.arange(depth_rows)).astype(jnp.float32),
        depth_cells,
    )
    spectrum = (
        prior_gain
        / (
            1.0
            + range_squared
            * (kappa_y[:, None, None] + kappa_z[None, :, None] + kappa_x[None, None, :])
        )
        ** 2
    )
    along_back = jnp.einsum("yzk,kx->yzx", along_freq * spectrum, cas_along, precision=highest)
    slab_block = lax.all_to_all(along_back, "space", split_axis=2, concat_axis=0, tiled=True)
    across_back = jnp.einsum("yzx,yk->xzk", slab_block, cas_across, precision=highest)
    depth_block = lax.all_to_all(across_back, "test", split_axis=2, concat_axis=1, tiled=True)
    result = jnp.einsum("xky,kz->xyz", depth_block, cas_depth, precision=highest)
    scale_back = 1.0 / (along_cells * width_cells * depth_cells)
    return result * scale_back


def dot3(a, b):
    def split(x):
        top = x.astype(jnp.bfloat16)
        return top, (x - top.astype(jnp.float32)).astype(jnp.bfloat16)

    def dot(x, y):
        return jnp.dot(x, y, preferred_element_type=jnp.float32)

    a_top, a_low = split(a)
    b_top, b_low = split(b)
    return dot(a_top, b_top) + (dot(a_top, b_low) + dot(a_low, b_top))


VM = pl.BlockSpec(memory_space=pltpu.VMEM)
SM = pl.BlockSpec(memory_space=pltpu.SMEM)
BIG = pltpu.CompilerParams(vmem_limit_bytes=60 * 1024 * 1024)


def shape(*dims, dtype=jnp.float32):
    return jax.ShapeDtypeStruct(dims, dtype)


def iotas(plane):
    return (
        lax.broadcasted_iota(jnp.int32, plane, 0),
        lax.broadcasted_iota(jnp.int32, plane, 1),
    )


def ring_sum(plane, edge):
    rows, lanes = plane.shape
    at_row, at_lane = iotas(plane.shape)
    up = jnp.where(at_row == rows - 1, edge, pltpu.roll(plane, rows - 1, 0))
    down = jnp.where(at_row == 0, edge, pltpu.roll(plane, 1, 0))
    right = jnp.where(at_lane == lanes - 1, edge, pltpu.roll(plane, lanes - 1, 1))
    left = jnp.where(at_lane == 0, edge, pltpu.roll(plane, 1, 1))
    return (up + down) + (right + left)


def plane_total(plane):
    rows, lanes = plane.shape
    return jnp.sum(plane.reshape(rows // 8, 8, lanes), axis=0)


def swap_blocks(planes):
    count = len(planes)
    lanes = planes[0].shape[1]
    block = lanes // count
    at_lane = iotas(planes[0].shape)[1] // block
    swapped = []
    for to in range(count):
        joined = planes[to]
        for frm in range(count):
            if frm != to:
                shift = (block * (frm - to)) % lanes
                joined = jnp.where(at_lane == frm, pltpu.roll(planes[frm], shift, 1), joined)
        swapped.append(joined)
    return swapped


def residual_kernel(
    spot, columns, logk, warm, before, after, observed, start, image, soft, sums, weighted, around
):
    rows, width, depth = logk.shape
    first_row, last_row = spot[0], spot[1]

    def prepare(to, logk_row, warm_row):
        soft_row = jnp.exp(0.5 * logk_row.astype(jnp.float32))
        soft[to] = soft_row
        weighted[to] = soft_row * warm_row.astype(jnp.float32)

    for i in range(3):
        prepare(i, before[i], before[3 + i])
        prepare(rows + 3 + i, after[i], after[3 + i])

    def fill(i, _):
        prepare(i + 3, logk[i], warm[i])
        return 0

    lax.fori_loop(0, rows, fill, 0)

    def first(i, _):
        row = first_row + i - 2
        inside = ((row >= 0) & (row < last_row)).astype(jnp.float32)
        soft_row = soft[i + 1]
        near = ring_sum(soft_row, 1.0) + (soft[i] + soft[i + 2])
        around[i] = near
        held = weighted[i + 1]
        beside = ring_sum(held, 0.0) + (weighted[i] + weighted[i + 2])
        start[i] = (soft_row * beside - held * near) * inside
        return 0

    lax.fori_loop(0, rows + 4, first, 0)

    def add(o, _):
        column = columns[0, o]
        row = column // width
        place = column - row * width
        local = row - first_row + 2

        @pl.when((local >= 0) & (local < rows + 4))
        def _():
            start[local, pl.ds(place, 1), :] += observed[pl.ds(o, 1), :]

        return 0

    lax.fori_loop(0, columns.shape[1], add, 0)

    def scale(i, _):
        weighted[i] = soft[i + 1] * start[i]
        return 0

    lax.fori_loop(0, rows + 4, scale, 0)

    def second(i, carry):
        total_rr, total_rq = carry
        row = first_row + i - 1
        inside = ((row >= 0) & (row < last_row)).astype(jnp.float32)
        held = weighted[i + 1]
        beside = ring_sum(held, 0.0) + (weighted[i] + weighted[i + 2])
        applied = (held * around[i + 1] - soft[i + 2] * beside) * inside
        image[i] = applied
        value = start[i + 1]
        own = ((i >= 1) & (i <= rows)).astype(jnp.float32)
        return (
            total_rr + own * plane_total(value * value),
            total_rq + own * plane_total(value * applied),
        )

    zero = jnp.zeros((8, depth), jnp.float32)
    total_rr, total_rq = lax.fori_loop(0, rows + 2, second, (zero, zero))
    sums[0] = total_rr
    sums[1] = total_rq


def face_terms(soft, field, head, axis):
    size = soft.shape[axis]
    at = iotas(soft.shape)[axis]
    both = field * head
    ahead = size - 1
    product = (field - pltpu.roll(field, ahead, axis)) * (head - pltpu.roll(head, ahead, axis))
    upper = jnp.where(at == size - 1, both, pltpu.roll(soft, ahead, axis) * product)
    lower = jnp.where(at == 0, both, pltpu.roll(soft * product, 1, axis))
    return upper + lower


MESH = pl.DeviceIdType.MESH


def greet(others):
    barrier = pltpu.get_barrier_semaphore()
    for other in others:
        pl.semaphore_signal(barrier, inc=1, device_id=other, device_id_type=MESH)
    pl.semaphore_wait(barrier, len(others))


def gradient_kernel(
    spot,
    sums,
    warm,
    heads,
    before,
    after,
    start,
    image,
    soft,
    cas,
    out,
    field,
    head,
    mine,
    from_mate,
    from_across,
    send_mate,
    take_mate,
    send_across,
    take_across,
    shared,
    send_sum,
    take_sum,
):
    rows, width, depth = warm.shape
    slabs = shared.shape[1]
    slab = lax.axis_index("space")
    others = [{"space": lax.rem(slab + k, slabs)} for k in range(1, slabs)]
    here = lax.axis_index("test")
    half, core = here // 2, lax.rem(here, 2)
    mate = {"test": 2 * half + 1 - core}
    across = {"test": 2 * (1 - half) + core}
    greet(others + [mate, across])
    first_row = spot[0]
    well = spot[2]

    def share(turn):
        return [
            pltpu.make_async_remote_copy(
                src_ref=shared.at[turn, slab],
                dst_ref=shared.at[turn, slab],
                send_sem=send_sum.at[turn, k],
                recv_sem=take_sum.at[turn, k],
                device_id=other,
                device_id_type=MESH,
            )
            for k, other in enumerate(others)
        ]

    def gathered_sum(turn, n):
        total = shared[turn, 0, n]
        for m in range(1, slabs):
            total = total + shared[turn, m, n]
        return jnp.broadcast_to(jnp.sum(total, axis=(0, 1), keepdims=True), (1, depth))

    shared[0, slab] = sums[...]
    for copy in share(0):
        copy.start()
    head[0] = before[6]
    head[rows + 1] = after[6]

    def keep_head(i, _):
        head[i + 1] = heads[i]
        return 0

    lax.fori_loop(0, rows, keep_head, 0)
    for copy in share(0):
        copy.wait()
    norm, curve = gathered_sum(0, 0), gathered_sum(0, 1)
    length = norm / curve

    def scale(i, _):
        field[i] = soft[i + 2] * (start[i + 1] - length * image[i])
        return 0

    lax.fori_loop(0, rows + 2, scale, 0)

    def apply(i, carry):
        total_rr, total_rq = carry
        held = field[i + 1]
        beside = ring_sum(held, 0.0) + (field[i] + field[i + 2])
        near = ring_sum(soft[i + 3], 1.0) + (soft[i + 2] + soft[i + 4])
        value = start[i + 2] - length * image[i + 1]
        applied = held * near - soft[i + 3] * beside
        return total_rr + plane_total(value * value), total_rq + plane_total(value * applied)

    zero = jnp.zeros((8, depth), jnp.float32)
    total_rr, total_rq = lax.fori_loop(0, rows, apply, (zero, zero))
    shared[1, slab, 0] = total_rr
    shared[1, slab, 1] = total_rq
    for copy in share(1):
        copy.start()
    for copy in share(1):
        copy.wait()
    norm_next, curve_next = gathered_sum(1, 0), gathered_sum(1, 1)
    ratio = norm_next / norm
    length_next = norm_next / (curve_next - ratio * norm_next / length)
    with_start = length + length_next * (1.0 + ratio)
    with_image = length_next * length

    def fill(to, warm_row):
        field[to] = (
            warm_row.astype(jnp.float32) + with_start * start[to + 1] - with_image * image[to]
        )

    fill(0, before[5])
    fill(rows + 1, after[3])

    def middle(i, _):
        fill(i + 1, warm[i])
        return 0

    lax.fori_loop(0, rows, middle, 0)
    at_row = iotas((width, depth))[0]
    count = 4
    groups = rows // count

    def term(i):
        s, f, h = soft[i + 3], field[i + 1], head[i + 1].astype(jnp.float32)
        gathered = face_terms(s, f, h, 0) + face_terms(s, f, h, 1)
        gathered += soft[i + 2] * ((f - field[i]) * (h - head[i].astype(jnp.float32)))
        gathered += soft[i + 4] * ((f - field[i + 2]) * (h - head[i + 2].astype(jnp.float32)))
        keep = at_row != well - (first_row + i) * width
        value = jnp.where(keep, -0.5 * s * gathered, 0.0)
        return dot3(value, cas[...])

    def to_mate(g):
        return pltpu.make_async_remote_copy(
            src_ref=mine.at[1 - core, g],
            dst_ref=from_mate.at[g],
            send_sem=send_mate.at[g],
            recv_sem=take_mate.at[g],
            device_id=mate,
            device_id_type=MESH,
        )

    def to_across(g):
        return pltpu.make_async_remote_copy(
            src_ref=mine.at[core, g, 1 - half],
            dst_ref=from_across.at[g],
            send_sem=send_across.at[g],
            recv_sem=take_across.at[g],
            device_id=across,
            device_id_type=MESH,
        )

    def group(g):
        for t, plane in enumerate(swap_blocks([term(g * count + p) for p in range(count)])):
            mine[t % 2, g, t // 2] = plane
        to_mate(g).start()

    def relay(g):
        to_mate(g).wait_recv()
        mine[core, g, 1 - half] += from_mate[g, 1 - half]
        to_across(g).start()

    group(0)

    def step(g, _):
        group(g)
        relay(g - 1)
        return 0

    lax.fori_loop(1, groups, step, 0)
    relay(groups - 1)

    def finish(g, _):
        to_across(g).wait_recv()
        out[g] = (mine[core, g, half] + from_mate[g, half]) + from_across[g]
        to_mate(g).wait_send()
        to_across(g).wait_send()
        return 0

    lax.fori_loop(0, groups, finish, 0)


def spectral_kernel(
    summed,
    tables,
    cas_across,
    cas_depth,
    out,
    freq,
    moments,
    filtered,
    going,
    coming,
    send_end,
    take_end,
    send_back,
    take_back,
):
    groups, width, lanes = summed.shape
    count, part = going.shape[0], going.shape[2]
    rows = groups * count
    slabs = moments.shape[0]
    slab, here = lax.axis_index("space"), lax.axis_index("test")
    others = [{"space": lax.rem(slab + k, slabs)} for k in range(1, slabs)]
    peers = [lax.rem(here + k, count) for k in range(1, count)]
    greet(others + [{"test": peer} for peer in peers])

    def mix(g, _):
        mixed = dot3(cas_across[...], summed[g])
        blocks = [mixed[j * part : (j + 1) * part] for j in range(count)]
        for p, plane in enumerate(swap_blocks(blocks)):
            freq[g * count + p] = plane
        return 0

    lax.fori_loop(0, groups, mix, 0)
    pole, level, slope, decay, wrap_one, wrap_two = (tables[n] for n in range(6))

    def walk(i, carry):
        one, two, back_one, back_two = carry
        value, back = freq[i], freq[rows - 1 - i]
        return (
            value + pole * one,
            pole * (two + one),
            back + pole * back_one,
            pole * (back_two + back_one),
        )

    zero = jnp.zeros((part, lanes), jnp.float32)
    ends = lax.fori_loop(0, rows, walk, (zero, zero, zero, zero))
    for n in range(4):
        moments[slab, n] = ends[n]
    copies = [
        pltpu.make_async_remote_copy(
            src_ref=moments.at[slab],
            dst_ref=moments.at[slab],
            send_sem=send_end.at[k],
            recv_sem=take_end.at[k],
            device_id=other,
            device_id_type=MESH,
        )
        for k, other in enumerate(others)
    ]
    for copy in copies:
        copy.start()
    for copy in copies:
        copy.wait()

    def carried(direction, n):
        one, two = zero, zero
        for m in range(slabs, 0, -1):
            other = lax.rem(slab + 2 * slabs - direction * m, slabs)
            one, two = (
                decay * one + moments[other, n],
                decay * (two + rows * one) + moments[other, n + 1],
            )
        return wrap_one * one, wrap_one * two + wrap_two * one

    def forward(i, carry):
        one, two = carry
        two = pole * (two + one)
        one = freq[i] + pole * one
        filtered[i] = level * one + slope * two
        return one, two

    lax.fori_loop(0, rows, forward, carried(1, 0))

    def backward(i, carry):
        one, two = carry
        at = rows - 1 - i
        two = pole * (two + one)
        one = pole * one
        filtered[at] += level * one + slope * two
        return one + freq[at], two

    lax.fori_loop(0, rows, backward, carried(-1, 2))

    def to_peer(k, g):
        return pltpu.make_async_remote_copy(
            src_ref=going.at[peers[k], g],
            dst_ref=coming.at[here, g],
            send_sem=send_back.at[k, g],
            recv_sem=take_back.at[k, g],
            device_id={"test": peers[k]},
            device_id_type=MESH,
        )

    def unmix(g, _):
        blocks = swap_blocks([filtered[g * count + p] for p in range(count)])
        stacked = jnp.concatenate(blocks, axis=0)
        mixed = dot3(cas_across[...], stacked)
        for u in range(count):
            going[u, g] = mixed[u * part : (u + 1) * part]
        for k in range(count - 1):
            to_peer(k, g).start()
        coming[here, g] = going[here, g]
        return 0

    lax.fori_loop(0, groups, unmix, 0)

    def back(g, _):
        for k in range(count - 1):
            to_peer(k, g).wait()
        for p, plane in enumerate(swap_blocks([coming[t, g] for t in range(count)])):
            out[g * count + p] = dot3(plane, cas_depth[...])
        return 0

    lax.fori_loop(0, groups, back, 0)


def table(length):
    indices = np.arange(length)
    angles = (indices[:, None] * indices[None, :] % length) * (2.0 * np.pi / length)
    return jnp.asarray((np.cos(angles) + np.sin(angles)).astype(np.float32))


def fast(log_k, heads, warm_adjoint, obs_columns, obs_residuals, well_columns):
    rows, width, depth = log_k.shape
    slabs = lax.axis_size("space")
    count = lax.axis_size("test")
    along = rows * slabs
    part = width // count
    block = depth // count
    first_row = lax.axis_index("space") * rows
    warm, head = warm_adjoint[0], heads[0]
    low = jnp.concatenate([log_k[:3], warm[:3], head[:1]])
    high = jnp.concatenate([log_k[rows - 3 :], warm[rows - 3 :], head[rows - 1 :]])
    before = lax.ppermute(high, "space", [(i, i + 1) for i in range(slabs - 1)])
    after = lax.ppermute(low, "space", [(i + 1, i) for i in range(slabs - 1)])
    spot = jnp.stack([first_row, jnp.int32(along), well_columns[0]]).astype(jnp.int32)
    start, image, soft, sums = pl.pallas_call(
        residual_kernel,
        out_shape=[
            shape(rows + 4, width, depth),
            shape(rows + 2, width, depth),
            shape(rows + 6, width, depth),
            shape(2, 8, depth),
        ],
        in_specs=[SM, SM, VM, VM, VM, VM, VM],
        out_specs=[VM] * 4,
        scratch_shapes=[
            pltpu.VMEM((rows + 6, width, depth), jnp.float32),
            pltpu.VMEM((rows + 4, width, depth), jnp.float32),
        ],
        compiler_params=BIG,
        name="residual",
    )(spot, obs_columns, log_k, warm, before, after, obs_residuals[0])
    cas_depth = table(depth)
    cas_across = table(width)
    groups = rows // count
    summed = pl.pallas_call(
        gradient_kernel,
        out_shape=shape(groups, width, depth),
        in_specs=[SM] + [VM] * 9,
        out_specs=VM,
        scratch_shapes=[
            pltpu.VMEM((rows + 2, width, depth), jnp.float32),
            pltpu.VMEM((rows + 2, width, depth), jnp.bfloat16),
            pltpu.VMEM((2, groups, 2, width, depth), jnp.float32),
            pltpu.VMEM((groups, 2, width, depth), jnp.float32),
            pltpu.VMEM((groups, width, depth), jnp.float32),
        ]
        + [pltpu.SemaphoreType.DMA((groups,))] * 4
        + [pltpu.VMEM((2, slabs, 2, 8, depth), jnp.float32)]
        + [pltpu.SemaphoreType.DMA((2, slabs - 1))] * 2,
        compiler_params=pltpu.CompilerParams(
            vmem_limit_bytes=60 * 1024 * 1024, collective_id=1, has_side_effects=True
        ),
        name="gradient",
    )(spot, sums, warm, head, before, after, start, image, soft, cas_depth)
    lanes_at = jnp.arange(depth)
    across_at = (lanes_at // block)[None, :] * part + jnp.arange(part)[:, None]
    depth_at = lax.axis_index("test") * block + lanes_at % block
    shift = 1.0 + range_squared * (
        kappa_of(across_at.astype(jnp.float32), width)
        + kappa_of(depth_at.astype(jnp.float32), depth)[None, :]
    )
    centre = 1.0 + shift / (2.0 * range_squared)
    pole = 1.0 / (centre + jnp.sqrt(centre * centre - 1.0))
    square = pole * pole
    gain = prior_gain / (range_squared * range_squared) * square / (width * depth)
    slope = gain / (1.0 - square) ** 2
    level = slope * (1.0 + square) / (1.0 - square)
    turn = pole**along
    wrap_one = 1.0 / (1.0 - turn)
    tables = jnp.stack(
        [pole, level, slope, pole**rows, wrap_one, along * turn * wrap_one * wrap_one]
    )
    return pl.pallas_call(
        spectral_kernel,
        out_shape=shape(rows, part, depth),
        in_specs=[VM] * 4,
        out_specs=VM,
        scratch_shapes=[
            pltpu.VMEM((rows, part, depth), jnp.float32),
            pltpu.VMEM((slabs, 4, part, depth), jnp.float32),
            pltpu.VMEM((rows, part, depth), jnp.float32),
            pltpu.VMEM((count, groups, part, depth), jnp.float32),
            pltpu.VMEM((count, groups, part, depth), jnp.float32),
            pltpu.SemaphoreType.DMA((slabs - 1,)),
            pltpu.SemaphoreType.DMA((slabs - 1,)),
            pltpu.SemaphoreType.DMA((count - 1, groups)),
            pltpu.SemaphoreType.DMA((count - 1, groups)),
        ],
        compiler_params=pltpu.CompilerParams(
            vmem_limit_bytes=40 * 1024 * 1024, collective_id=2, has_side_effects=True
        ),
        name="spectral",
    )(summed, tables, cas_across, cas_depth)


def pick(log_k, *rest):
    rows, width, depth = log_k.shape
    count = lax.axis_size("test")
    fits = depth == 128 and count == 4 and rows % count == 0 and width % (8 * count) == 0
    return (fast if fits and lax.axis_size("space") > 1 else on_device)(log_k, *rest)


def solution(mesh):
    placed = (
        P(("groups", "space"), None, None),
        P("test", ("groups", "space"), None, None),
        P("test", ("groups", "space"), None, None),
        P("test", "groups"),
        P("test", "groups", None),
        P(("groups", "test")),
    )
    return jax.shard_map(
        pick,
        mesh=mesh,
        in_specs=placed,
        out_specs=P(("groups", "space"), "test", None),
        check_vma=False,
    )
```
